256 devices in a mesh: feat: 8 (over x, z_hi), store: 32 (over y, z_lo, core).
Axes of the slice: x: 4, y: 4, z: 8 (z_hi: 2, z_lo: 4; z = z_hi * 4 + z_lo), core: 2. Of those that a mesh axis runs over, the one named last changes fastest.
Arguments:
- layer_input: bfloat16 [16384, 8192], P('store', 'feat'), may hold values from -6 to 6
- out_grad: bfloat16 [16384, 8192], P('store', 'feat'), may hold values from -6 to 6
- proj_in: bfloat16 [8192, 256], P('feat'), may hold values from -0.0625 to 0.0625
- proj_out: bfloat16 [8192, 256], P('feat'), may hold values from -0.0625 to 0.0625
- inv_diag: float32 [65536], P('feat'), may hold values from 0.1 to 10
- stored: float32 [6144, 65536], P('store', 'feat'), may hold values from -0.0014648438 to 0.0014648438
- seq_lengths: int32 [32, 16], P('store'), may hold values from 1 to 64, 512 in all within a row
- query_order: int32 [32, 16], P('store'), may hold values from 0 to 15, as said below
Outputs:
- scores: float32 [512, 6144], P('feat', 'store')
The draws below stay inside these ranges and needn't reach their ends.
Inputs may be any that keep to these rules, and one draw needn't show every extreme that they name: `query_order`: each row is an ordering of the query slots 0 to 15, each slot once.
All inputs are finite; a program needn't handle non-finite values.
Results may differ from the reference program's by a relative error of at most 0.0003.
Values sent between devices are 32-bit elements; how exact they have to be, the bound alone decides.
A program may use at most 64 MiB of HBM per device.

```python
import math
import jax
import jax.numpy as jnp
import numpy as np
from jax import lax

D = 8192
PIN = 256
POUT = 256
FEATS = 65536
TOK_DEV = 512
Q_DEV = 16
LMAX = 64
NBLK = 32
NTOK = 16384
NQ = 512
ROWS = 6144


def draw_query_order(key, part):
    keys = jax.random.split(jax.random.fold_in(key, 7), NBLK)
    orders = jax.vmap(lambda single: jax.random.permutation(single, Q_DEV))(keys)
    return orders.astype(jnp.int32)


def block_scale(stream_key, extent, cuts, least, top_value):
    def one(axis_at, shards_of):
        draws = jax.random.uniform(jax.random.fold_in(jax.random.fold_in(stream_key, 6), axis_at), (shards_of,), jnp.float32, least / len(cuts), top_value / len(cuts))
        return jnp.repeat(jnp.exp(draws), extent[axis_at] // shards_of).reshape((-1,) + (1,) * (len(extent) - axis_at - 1))

    factor_of = one(*cuts[0])
    for cut in cuts[1:]:
        factor_of = factor_of * one(*cut)
    return factor_of


def split_up(count, total, most, slope):
    weights = [(1 << 20) // math.isqrt(rank ** slope) + 1 for rank in range(2, count + 1)]
    rest, given = total - most - (count - 1), [1] * (count - 1)
    while rest > 0:
        free = [i for i in range(count - 1) if given[i] < most]
        whole, budget = sum([weights[i] for i in free]), rest
        for i in free:
            extra = min(most - given[i], max(1, budget * weights[i] // whole), rest)
            given[i] = given[i] + extra
            rest = rest - extra
    return np.array([most] + given)


def ragged_sizes(key, number_of, total, limit, lean):
    if number_of == 2:
        one = jax.random.randint(key, (), max(1, total - limit), min(limit, total - 1) + 1)
        return jnp.stack([one, total - one])
    tallies = jnp.asarray(split_up(number_of, total, limit, lean), jnp.int32)
    couples = (number_of - 1) // 2
    donor, sink = tallies[1:1 + 2 * couples:2], tallies[2:2 + 2 * couples:2]
    margin = jnp.minimum(donor - 1, limit - sink)
    shifted = jax.random.randint(jax.random.fold_in(key, 1), (couples,), 0, 1 << 20) % (margin + 1)
    tallies = tallies.at[1:1 + 2 * couples:2].set(donor - shifted).at[2:2 + 2 * couples:2].set(sink + shifted)
    return tallies[jax.random.permutation(jax.random.fold_in(key, 2), number_of)]


def normal_values(key, shape, deviation, most, shards=(), held_as=jnp.bfloat16):
    array = jax.random.normal(key, shape, jnp.float32) * deviation
    if len(shards) > 0:
        array = block_scale(key, shape, shards, -0.22, 0.18) * array
    return jnp.clip(array, min=-most, max=most).astype(held_as)


def setup_inputs(seed: int = 0) -> dict:
    streams_of = jax.random.split(jax.random.key(seed), 9)
    layer_input = normal_values(streams_of[0], (NTOK, D), 1.0, 6.0, ((0, 32), (1, 8)))
    out_grad = normal_values(streams_of[1], (NTOK, D), 1.0, 6.0, ((0, 32), (1, 8)))
    proj_in = normal_values(streams_of[2], (D, PIN), D ** -0.5, 0.0625, ((0, 8),))
    proj_out = normal_values(streams_of[3], (D, POUT), D ** -0.5, 0.0625, ((0, 8),))
    inv_diag = jnp.clip(jnp.exp(math.log(10.0) - 4.6051702 * jax.random.uniform(streams_of[4], (FEATS,), jnp.float32) ** block_scale(streams_of[4], (FEATS,), ((0, 8),), -0.2, 0.2)), 0.1, 10.0)
    stored = normal_values(streams_of[5], (ROWS, FEATS), (FEATS * 256) ** -0.5, 0.0014648438, ((0, 32), (1, 8)), jnp.float32)
    seq_lengths = jax.vmap(lambda own: ragged_sizes(own, Q_DEV, TOK_DEV, LMAX, 2))(jax.random.split(streams_of[6], NBLK)).reshape((NBLK, Q_DEV)).astype(jnp.int32)
    query_order = draw_query_order(jax.random.fold_in(streams_of[8], 71), 0)
    return dict(layer_input=layer_input, out_grad=out_grad, proj_in=proj_in, proj_out=proj_out, inv_diag=inv_diag, stored=stored, seq_lengths=seq_lengths, query_order=query_order)


def slot_matrix(lengths_row, order_row, count):
    ends = jnp.cumsum(lengths_row).astype(jnp.int32)
    position = jnp.arange(count, dtype=jnp.int32)
    segment = jnp.sum((position[:, None] >= ends[None, :]).astype(jnp.int32), axis=1)
    slots = jnp.arange(Q_DEV, dtype=jnp.int32)
    onehot = (segment[None, :] == slots[:, None]).astype(jnp.float32)
    mapping = (order_row[None, :] == slots[:, None]).astype(jnp.float32)
    return jnp.dot(mapping, onehot, precision=lax.Precision.HIGHEST)


def reference(layer_input, out_grad, proj_in, proj_out, inv_diag, stored, seq_lengths, query_order):
    inputs = layer_input.reshape(NBLK, TOK_DEV, D)
    grads = out_grad.reshape(NBLK, TOK_DEV, D)

    def one_block(packed):
        block_in, block_grad, lengths_row, order_row = packed
        in_proj = jnp.dot(block_in, proj_in, preferred_element_type=jnp.float32)
        grad_proj = jnp.dot(block_grad, proj_out, preferred_element_type=jnp.float32)
        member = slot_matrix(lengths_row, order_row, TOK_DEV)
        masked = member[:, :, None] * in_proj[None, :, :]
        query_grad = jnp.einsum("qti,tj->qij", masked, grad_proj, precision=lax.Precision.HIGHEST)
        query_grad = query_grad.reshape(Q_DEV, FEATS) * inv_diag[None, :]
        return jnp.einsum("qf,rf->qr", query_grad, stored, precision=lax.Precision.HIGHEST)

    result = lax.map(one_block, (inputs, grads, seq_lengths, query_order))
    return result.reshape(NQ, ROWS)
```

```python
import heapq

import jax
import jax.numpy as jnp
from jax import lax
from jax.experimental import pallas as pl
from jax.experimental.pallas import tpu as pltpu
from jax.sharding import PartitionSpec as P

MESH = pl.DeviceIdType.MESH
F32, BF16 = jnp.float32, jnp.bfloat16
NX, NY, NZ = 4, 4, 8
QB = 16
A0, B0, C0, TOK = 0, 16, 40, 64
INROWS = 40


def place():
    f, s = lax.axis_index("feat"), lax.axis_index("store")
    return f // 2, s // 8, (f % 2) * 4 + (s // 2) % 4, s % 2


def device(x, y, z, c):
    x, y, z, c = x % NX, y % NY, z % NZ, c % 2
    return (x * 2 + z // 4, y * 8 + (z % 4) * 2 + c)


class Message:
    def __init__(self, name, deps, kb, axis, hop, ref):
        self.name, self.deps, self.kb, self.axis, self.hop, self.ref = name, deps, kb, axis, hop, ref


def gather_plan(me, grads, ins):
    x, y, z, c = me
    out = []

    def zz(v):
        return v % 4, (v % NZ) // 4

    def add(name, deps, kb, axis, hop, ref):
        out.append(Message(name, tuple(deps), kb, axis, hop, ref))

    def ga(zv, ys=slice(None)):
        lo, hi = zz(zv)
        return grads.at[ys, lo, :, hi, A0:B0, :]

    def gb(zv, xv, ys=slice(None)):
        lo, hi = zz(zv)
        return grads.at[ys, lo, xv % NX, hi, B0:C0, :]

    def gc(xv, yv, zs=slice(None)):
        return grads.at[yv % NY, zs, xv % NX, :, C0:TOK, :]

    first, second = pl.ds(0, 2), pl.ds(2, 2)
    lo, hi = zz(z)
    for k in (1, 2, 3, 4):
        for sign in (1, -1):
            zlo, zhi = zz(z - sign * (k - 1))
            cols = slice(None) if k < 4 else pl.ds(0 if sign > 0 else 128, 128)
            deps = ["g"] if k == 1 else [f"Cz{sign * (k - 1)}"]
            add(f"Cz{sign * k}", deps, 24 if k < 4 else 12, "z", sign, grads.at[y, zlo, x, zhi, C0:TOK, cols])
    call = [f"Cz{s * k}" for k in (1, 2, 3, 4) for s in (1, -1)]
    for sign in (1, -1):
        add(f"Cx{sign}", ["g"] + call, 192, "x", sign, gc(x, y))
    for sign in (1, -1):
        add(f"Cx{2 * sign}", [f"Cx{sign}"], 96, "x", sign, gc(x - sign, y, first if sign > 0 else second))
    for hop in (1, -1, 2):
        add(f"By{hop}", ["g"], 24, "y", hop, grads.at[y, lo, x, hi, B0:C0, :])
    ball = ["g"] + [f"By{h}" for h in (1, -1, 2)]
    for k in (1, 2, 3, 4):
        for sign in (1, -1):
            deps = ball if k == 1 else [f"Bz{sign * (k - 1)}"]
            ys = slice(None) if k < 4 else (first if sign > 0 else second)
            add(f"Bz{sign * k}", deps, 96 if k < 4 else 48, "z", sign, gb(z - sign * (k - 1), x, ys))
    for hop in (1, -1, 2):
        add(f"Ax{hop}", ["g"], 16, "x", hop, grads.at[y, lo, x, hi, A0:B0, :])
    aall = ["g"] + [f"Ax{h}" for h in (1, -1, 2)]
    for hop in (1, -1, 2):
        add(f"Ay{hop}", aall, 64, "y", hop, grads.at[y, lo, :, hi, A0:B0, :])
    for k in (1, 2, 3):
        add(f"Iz{k}", ["i"], 80, "i", k, ins.at[y, lo])
    iall = ["i"] + [f"Iz{k}" for k in (1, 2, 3)]
    for sign in (1, -1):
        add(f"Iy{sign}", iall, 320, "y", sign, ins.at[y])
    for sign in (1, -1):
        add(f"Iy{2 * sign}", [f"Iy{sign}"], 160, "y", sign, ins.at[(y - sign) % NY, first if sign > 0 else second])
    for d in (0, -1, 1, -2, 2, -3, 3, 4):
        if d == 0:
            deps = ball
        elif d == 4:
            deps = ["Bz4", "Bz-4"]
        else:
            deps = [f"Bz{-d}"]
        for sign in (1, -1):
            add(f"Bx{d},{sign}", deps, 96, "x", sign, gb(z + d, x))
        for sign in (1, -1):
            add(f"Bx{d},{2 * sign}", [f"Bx{d},{sign}"], 48, "x", sign, gb(z + d, x - sign, first if sign > 0 else second))
    for d in (0, -1, 1, 2):
        deps = (["g"] + call) if d == 0 else (["Cx2", "Cx-2"] if d == 2 else [f"Cx{-d}"])
        for sign in (1, -1):
            add(f"Cy{d},{sign}", deps, 192, "y", sign, gc(x + d, y))
        for sign in (1, -1):
            add(f"Cy{d},{2 * sign}", [f"Cy{d},{sign}"], 96, "y", sign, gc(x + d, y - sign, first if sign > 0 else second))
    yall = aall + [f"Ay{h}" for h in (1, -1, 2)]
    for k in (1, 2, 3, 4):
        for sign in (1, -1):
            deps = yall if k == 1 else [f"Az{sign * (k - 1)}"]
            ys = slice(None) if k < 4 else (first if sign > 0 else second)
            add(f"Az{sign * k}", deps, 256 if k < 4 else 128, "z", sign, ga(z - sign * (k - 1), ys))
    return out


def target(me, m):
    x, y, z, c = me
    if m.axis == "x":
        return device(x + m.hop, y, z, c)
    if m.axis == "y":
        return device(x, y + m.hop, z, c)
    if m.axis == "z":
        return device(x, y, z + m.hop, c)
    return device(x, y, (z // 4) * 4 + (z % 4 + m.hop) % 4, c)


def order_of(plan, late=8.0):
    rate, latency = 42.0, 1.5
    free, got, sent, events, steps = {}, set(), set(), [(0.0, 0, "g"), (late, 1, "i")], []
    heapq.heapify(events)
    count = 2
    while events:
        now, _, name = heapq.heappop(events)
        got.add(name)
        steps.append(("wait", name))
        for m in plan:
            if m.name in sent or not all(d in got for d in m.deps):
                continue
            sent.add(m.name)
            steps.append(("send", m.name))
            if m.axis == "i":
                links, kb = ("z+", "z-"), m.kb
            elif abs(m.hop) > 1:
                links, kb = (m.axis + "+", m.axis + "-"), m.kb
            else:
                links, kb = ((m.axis + "+",) if m.hop > 0 else (m.axis + "-",)), m.kb
            end = max(now, *(free.get(k, 0.0) for k in links)) + kb / rate
            for k in links:
                free[k] = end
            heapq.heappush(events, (end + latency, count, m.name))
            count += 1
    return steps


def split(v):
    high = v.astype(BF16)
    return high, (v - high.astype(F32)).astype(BF16)


def dot3(a, b, dims):
    (ah, al), (bh, bl) = a, b
    return (
        lax.dot_general(ah, bh, dims, preferred_element_type=F32)
        + lax.dot_general(ah, bl, dims, preferred_element_type=F32)
        + lax.dot_general(al, bh, dims, preferred_element_type=F32)
    )


RS = ("R1", "L1", "R1b", "L1b", "R2", "L2", "Z")


def kernel(
    li_hbm, og_hbm, pi_hbm, po_hbm, inv_hbm, st_hbm, len_ref, ord_ref, out_ref,
    li, og, pi, po, inv, raw, st_hi, st_lo, pg, pin, rg, rin, grads, ins, q_hi, q_lo, sc, rsc, fin,
    load_sem, gsend, grecv, rsend, rrecv, ssend, srecv, fsend, frecv,
):
    me = x, y, z, c = place()
    zlo, zhi = z % 4, z // 4
    loads = [
        pltpu.make_async_copy(src, dst, load_sem.at[n])
        for n, (src, dst) in enumerate(
            ((og_hbm, og), (po_hbm, po), (li_hbm, li), (pi_hbm, pi), (inv_hbm, inv), (st_hbm, raw.at[c]))
        )
    ]
    for copy in loads:
        copy.start()
    line = [device(x, y, zhi * 4 + (zlo + k) % 4, c) for k in (1, 2, 3)]
    partners = [
        device(x + 1, y, z, c), device(x - 1, y, z, c), device(x + 2, y, z, c),
        device(x, y + 1, z, c), device(x, y - 1, z, c), device(x, y + 2, z, c),
        device(x, y, z + 1, c), device(x, y, z - 1, c), device(x, y, z + 4, c),
        device(x, y, z, c + 1), device(x, y, z + 4, c + 1), *line,
    ]
    barrier = pltpu.get_barrier_semaphore()
    for d in partners:
        pl.semaphore_signal(barrier, inc=1, device_id=d, device_id_type=MESH)
    pl.semaphore_wait(barrier, len(partners))

    def remote(src, dst, send, recv, d):
        return pltpu.make_async_remote_copy(src, dst, send, recv, device_id=d, device_id_type=MESH)

    right, left, core = device(x + 1, y, z, c), device(x - 1, y, z, c), device(x, y, z, c + 1)
    xr, xl, xo = (x + 1) % NX, (x - 1) % NX, (x + 2) % NX
    swap = remote(st_hbm, raw.at[c], fsend.at[3], frecv.at[3], core)

    def reduce_plan(n, buf, got):
        def one(k, src, d):
            return remote(src, got.at[k], rsend.at[n, k], rrecv.at[n, k], d)

        return {
            "R1": one(0, buf.at[xo, 0], right), "L1": one(1, buf.at[xo, 1], left),
            "R1b": one(2, buf.at[xr, 1], right), "L1b": one(3, buf.at[xl, 0], left),
            "R2": one(4, buf.at[xr, 0], right), "L2": one(5, buf.at[xl, 1], left),
            "Z": one(6, buf.at[x, 1 - zhi], device(x, y, z + 4, c)),
        }

    first, second = reduce_plan(0, pg, rg), reduce_plan(1, pin, rin)

    loads[0].wait()
    loads[1].wait()
    pg[...] = jnp.dot(og[...], po[...], preferred_element_type=F32).reshape(pg.shape)
    for k in ("R1", "L1", "R1b", "L1b"):
        first[k].start()
    loads[2].wait()
    loads[3].wait()
    pin[...] = lax.dot_general(
        pi[...], li[...], (((0,), (1,)), ((), ())), preferred_element_type=F32
    ).reshape(pin.shape)
    for k in ("R1", "L1", "R1b", "L1b"):
        second[k].start()
    swap.start()

    position = lax.broadcasted_iota(jnp.int32, (8, 512), 1)
    slots, begin = jnp.zeros((8, 512), F32), jnp.int32(0)
    for k in range(QB):
        end = begin + len_ref[0, k]
        here = (position >= begin) & (position < end)
        slots = slots + jnp.where(here, ord_ref[0, k], 0).astype(F32)
        begin = end
    ins[y, zlo, 32:40, :] = slots

    def halfway(cps, buf, got):
        cps["R1"].wait_recv()
        buf[xr, 0] = buf[xr, 0] + got[0]
        cps["R2"].start()
        cps["L1"].wait_recv()
        buf[xl, 1] = buf[xl, 1] + got[1]
        cps["L2"].start()

    def reduced(cps, buf, got):
        for k in ("R1b", "L1b", "R2", "L2"):
            cps[k].wait_recv()
        buf[x, 0] = buf[x, 0] + (got[3] + got[4])
        buf[x, 1] = buf[x, 1] + (got[2] + got[5])
        cps["Z"].start()

    halfway(first, pg, rg)
    halfway(second, pin, rin)
    reduced(first, pg, rg)
    reduced(second, pin, rin)

    plan = gather_plan(me, grads, ins)
    copies = {
        m.name: remote(m.ref, m.ref, gsend.at[n], grecv.at[n], target(me, m)) for n, m in enumerate(plan)
    }
    for verb, name in order_of(plan):
        if name == "g":
            first["Z"].wait_recv()
            grads[y, zlo, x, zhi] = pg[x, zhi] + rg[6]
        elif name == "i":
            second["Z"].wait_recv()
            ins[y, zlo, 0:32, :] = pin[x, zhi] + rin[6]
        elif verb == "send":
            copies[name].start()
        else:
            copies[name].wait_recv()

    loads[4].wait()
    loads[5].wait()
    swap.wait()

    @pl.loop(0, 16)
    def _(k):
        cols = pl.ds(pl.multiple_of(k * 512, 512), 512)
        for core_of in range(2):
            high, low = split(raw[core_of, :, cols] * inv[:, cols])
            st_hi[core_of, :, cols] = high
            st_lo[core_of, :, cols] = low

    @pl.loop(0, 16)
    def _(b):
        by, bz = b // 4, b % 4
        g = split(grads[by, bz].reshape(512, 256))
        mine = ins[by, bz]
        rows = mine[0:32, :]
        member = (mine[32:33, :] == lax.broadcasted_iota(jnp.int32, (QB, 512), 0).astype(F32)).astype(F32)
        high = rows.astype(BF16).astype(F32)
        masked = [
            (v[:, None, :] * member[None]).reshape(512, 512).astype(BF16) for v in (high, rows - high)
        ]
        high, low = split(dot3(masked, g, (((1,), (0,)), ((), ()))))
        at = pl.ds(pl.multiple_of(b * QB, QB), QB)
        for i in range(32):
            q_hi[at, i * 256:(i + 1) * 256] = high[i * QB:(i + 1) * QB]
            q_lo[at, i * 256:(i + 1) * 256] = low[i * QB:(i + 1) * QB]

    sc[...] = jnp.zeros_like(sc)

    @pl.loop(0, 8)
    def _(k):
        cols = pl.ds(pl.multiple_of(k * 1024, 1024), 1024)
        q = (q_hi[:, cols], q_lo[:, cols])
        for core_of in range(2):
            part = dot3(q, (st_hi[core_of, :, cols], st_lo[core_of, :, cols]), (((1,), (1,)), ((), ())))
            sc[:, :, core_of] = sc[:, :, core_of] + part.reshape(4, 2, 32, 192)

    sends = [
        remote(sc.at[(x + hop) % NX], rsc.at[n], ssend.at[n], srecv.at[n], device(x + hop, y, z, c))
        for n, hop in enumerate((1, -1, 2))
    ]
    for copy in sends:
        copy.start()
    for copy in sends:
        copy.wait_recv()
    sc[x] = sc[x] + (rsc[0] + rsc[1]) + rsc[2]
    ends = [
        remote(sc.at[x, 1 - zhi, c], fin.at[0], fsend.at[0], frecv.at[0], device(x, y, z + 4, c)),
        remote(sc.at[x, 1 - zhi, 1 - c], fin.at[1], fsend.at[1], frecv.at[1], device(x, y, z + 4, c + 1)),
        remote(sc.at[x, zhi, 1 - c], fin.at[2], fsend.at[2], frecv.at[2], core),
    ]
    for copy in ends:
        copy.start()
    for copy in ends:
        copy.wait_recv()
    mine = sc[x, zhi, c] + fin[0]
    theirs = fin[1] + fin[2]
    for half in range(2):
        part = slice(half * QB, (half + 1) * QB)
        out_ref[pl.ds(pl.multiple_of(half * 32 + c * QB, QB), QB), :] = mine[part]
        out_ref[pl.ds(pl.multiple_of(half * 32 + (1 - c) * QB, QB), QB), :] = theirs[part]

    for copy in (*first.values(), *second.values(), *copies.values(), *sends, *ends):
        copy.wait_send()


def body(layer_input, out_grad, proj_in, proj_out, inv_diag, stored, seq_lengths, query_order):
    count = 200
    hbm, smem = pl.BlockSpec(memory_space=pl.ANY), pl.BlockSpec(memory_space=pltpu.SMEM)
    dma = pltpu.SemaphoreType.DMA
    return pl.pallas_call(
        kernel,
        out_shape=jax.ShapeDtypeStruct((64, 192), F32),
        in_specs=[hbm] * 6 + [smem] * 2,
        out_specs=pl.BlockSpec(memory_space=pltpu.VMEM),
        scratch_shapes=[
            pltpu.VMEM((512, 1024), BF16),
            pltpu.VMEM((512, 1024), BF16),
            pltpu.VMEM((1024, 256), BF16),
            pltpu.VMEM((1024, 256), BF16),
            pltpu.VMEM((1, 8192), F32),
            pltpu.VMEM((2, 192, 8192), F32),
            pltpu.VMEM((2, 192, 8192), BF16),
            pltpu.VMEM((2, 192, 8192), BF16),
            pltpu.VMEM((4, 2, 64, 256), F32),
            pltpu.VMEM((4, 2, 32, 512), F32),
            pltpu.VMEM((7, 64, 256), F32),
            pltpu.VMEM((7, 32, 512), F32),
            pltpu.VMEM((4, 4, 4, 2, TOK, 256), F32),
            pltpu.VMEM((4, 4, INROWS, 512), F32),
            pltpu.VMEM((256, 8192), BF16),
            pltpu.VMEM((256, 8192), BF16),
            pltpu.VMEM((4, 2, 2, 32, 192), F32),
            pltpu.VMEM((3, 2, 2, 32, 192), F32),
            pltpu.VMEM((3, 32, 192), F32),
            dma((6,)),
            dma((96,)), dma((96,)),
            dma((2, 7)), dma((2, 7)),
            dma((3,)), dma((3,)),
            dma((4,)), dma((4,)),
        ],
        compiler_params=pltpu.CompilerParams(
            collective_id=0, has_side_effects=True, vmem_limit_bytes=60 * 2**20
        ),
    )(layer_input, out_grad, proj_in, proj_out, inv_diag.reshape(1, -1), stored, seq_lengths, query_order)


def solution(mesh):
    return jax.shard_map(
        body,
        mesh=mesh,
        in_specs=(
            P("store", "feat"),
            P("store", "feat"),
            P("feat", None),
            P("feat", None),
            P("feat"),
            P("store", "feat"),
            P("store", None),
            P("store", None),
        ),
        out_specs=P("feat", "store"),
        check_vma=False,
    )
```

```python
import heapq

import jax
import jax.numpy as jnp
from jax import lax
from jax.experimental import pallas as pl
from jax.experimental.pallas import tpu as pltpu
from jax.sharding import PartitionSpec as P

MESH = pl.DeviceIdType.MESH
F32, BF16 = jnp.float32, jnp.bfloat16
NX, NY, NZ = 4, 4, 8
QB = 16
A0, B0, C0, TOK = 0, 16, 40, 64
INROWS = 40


def place():
    f, s = lax.axis_index("feat"), lax.axis_index("store")
    return f // 2, s // 8, (f % 2) * 4 + (s // 2) % 4, s % 2


def device(x, y, z, c):
    x, y, z, c = x % NX, y % NY, z % NZ, c % 2
    return (x * 2 + z // 4, y * 8 + (z % 4) * 2 + c)


class Message:
    def __init__(self, name, deps, kb, axis, hop, ref):
        self.name, self.deps, self.kb, self.axis, self.hop, self.ref = name, tuple(deps), kb, axis, hop, ref


def ring(k, sign, tag):
    return f"{tag}{sign * k}"


def around(tag):
    return [ring(k, s, tag) for k in (1, 2, 3, 4) for s in (1, -1)]


NEAR, FAR = (0, 1, -1), 2


def gather_plan(me, grads, ins):
    x, y, z, c = me
    out = []

    def zz(v):
        return v % 4, (v % NZ) // 4

    def add(name, deps, kb, axis, hop, ref):
        out.append(Message(name, deps, kb, axis, hop, ref))

    def ga(zv, yv, xs=slice(None)):
        lo, hi = zz(zv)
        return grads.at[yv % NY, lo, xs, hi, A0:B0, :]

    def gb(zv, yv, xv):
        lo, hi = zz(zv)
        return grads.at[yv % NY, lo, xv % NX, hi, B0:C0, :]

    def gz(xv, yv, rows, zs=slice(None)):
        return grads.at[yv % NY, zs, xv % NX, :, rows, :]

    first, second = pl.ds(0, 2), pl.ds(2, 2)
    brows, crows = slice(B0, C0), slice(C0, TOK)
    ka, kb, kc = (B0 - A0), (C0 - B0), (TOK - C0)
    lo, hi = zz(z)
    from_y = {1: -1, -1: 1, 2: 2}
    for k in (1, 2, 3, 4):
        for sign in (1, -1):
            zlo, zhi = zz(z - sign * (k - 1))
            cols = slice(None) if k < 4 else pl.ds(0 if sign > 0 else 128, 128)
            deps = ["g"] if k == 1 else [ring(k - 1, sign, "Cz")]
            add(ring(k, sign, "Cz"), deps, kc if k < 4 else kc / 2, "z", sign, grads.at[y, zlo, x, zhi, crows, cols])
    call = ["g"] + around("Cz")
    for hop in (1, -1, 2):
        add(f"Ax{hop}", ["g"], ka, "x", hop, grads.at[y, lo, x, hi, A0:B0, :])
    aall = ["g"] + [f"Ax{h}" for h in (1, -1, 2)]
    for hop in (1, -1, 2):
        add(f"By{hop}", ["g"], kb, "y", hop, gb(z, y, x))
    for hop in (1, -1, 2):
        add(f"Ay{hop}", aall, 4 * ka, "y", hop, ga(z, y))
    for sign in (1, -1):
        add(f"Cx{sign}", call, 8 * kc, "x", sign, gz(x, y, crows))
    for sign in (1, -1):
        half = first if sign > 0 else second
        add(f"Cx{2 * sign}", [f"Cx{sign}"], 4 * kc, "x", sign, gz(x - sign, y, crows, half))
    for k in (1, 2, 3):
        add(f"Iz{k}", ["i", "Cz3", "Cz-3"], 80, "i", k, ins.at[y, lo])
    iall = ["i"] + [f"Iz{k}" for k in (1, 2, 3)]
    needs = {}
    for r in (*NEAR, FAR):
        tag = f"B{r}z"
        here = ["g"] if r == 0 else [f"By{from_y[r]}"]
        held = ["A0z2", "A0z-2"] if r == FAR else []
        for k in (1, 2, 3, 4):
            for sign in (1, -1):
                deps = here + held if k == 1 else [ring(k - 1, sign, tag)]
                zv = z - sign * (k - 1)
                ref = gb(zv, y + r, x)
                if k == 4:
                    zlo, zhi = zz(zv)
                    ref = grads.at[(y + r) % NY, zlo, x, zhi, brows, pl.ds(0 if sign > 0 else 128, 128)]
                add(ring(k, sign, tag), deps, kb if k < 4 else kb / 2, "z", sign, ref)
        ball = here + around(tag)
        brought = []
        if r == 0:
            for d in (0, -1, 1, -2, 2, -3, 3, 4):
                deps = ["g"] if d == 0 else ([ring(4, 1, tag), ring(4, -1, tag)] if d == 4 else [f"{tag}{-d}"])
                for sign in (1, -1):
                    add(f"B0x{sign},{d}", deps, kb, "x", sign, gb(z + d, y, x))
            came = {s: [f"B0x{s},{d}" for d in (0, -1, 1, -2, 2, -3, 3, 4)] for s in (1, -1)}
        else:
            for sign in (1, -1):
                add(f"B{r}x{sign}", ball + (["B1x1", "B1x-1"] if r == FAR else []), 8 * kb, "x", sign, gz(x, y + r, brows))
            came = {s: [f"B{r}x{s}"] for s in (1, -1)}
        for sign in (1, -1):
            half = first if sign > 0 else second
            add(f"B{r}x{2 * sign}", came[sign], 4 * kb, "x", sign, gz(x - sign, y + r, brows, half))
            brought += came[sign] + [f"B{r}x{2 * sign}"]
        tag = f"A{r}z"
        here = aall if r == 0 else [f"Ay{from_y[r]}"]
        held = ["A1z3", "A-1z3"] if r == FAR else ["B1z3", "B1z-3"]
        for k in (1, 2, 3, 4):
            for sign in (1, -1):
                deps = here + held if k == 1 else [ring(k - 1, sign, tag)]
                xs = slice(None) if k < 4 else (first if sign > 0 else second)
                ref = ga(z - sign * (k - 1), y + r, xs)
                add(ring(k, sign, tag), deps, 4 * ka if k < 4 else 2 * ka, "z", sign, ref)
        needs[r] = ball + brought + here + around(tag)
        if r == 0:
            needs[r] += call + ["Cx1", "Cx-1", "Cx2", "Cx-2"] + iall
            for d in (0, -1, 1, 2):
                deps = call if d == 0 else (["Cx2", "Cx-2"] if d == 2 else [f"Cx{-d}"])
                for sign in (1, -1):
                    add(f"C{d}y{sign}", deps, 8 * kc, "y", sign, gz(x + d, y, crows))
            for sign in (1, -1):
                add(f"Iy{sign}", iall, 320, "y", sign, ins.at[y])
        elif r != FAR:
            sign = from_y[r]
            needs[r] += [f"C{d}y{sign}" for d in (0, -1, 1, 2)] + [f"Iy{sign}"]
        else:
            for sign in (1, -1):
                half = first if sign > 0 else second
                add(f"Iy{2 * sign}", [f"Iy{sign}", f"C2y{sign}"], 160, "y", sign, ins.at[(y - sign) % NY, half])
                needs[r] += [f"Iy{2 * sign}"]
            for d in (0, -1, 1, 2):
                for sign in (1, -1):
                    half = first if sign > 0 else second
                    deps = [f"C{d}y{sign}", f"C1y{sign}"]
                    add(f"C{d}y{2 * sign}", deps, 4 * kc, "y", sign, gz(x + d, y - sign, crows, half))
                    needs[r] += [f"C{d}y{2 * sign}"]
    return out, needs


def target(me, m):
    x, y, z, c = me
    if m.axis == "x":
        return device(x + m.hop, y, z, c)
    if m.axis == "y":
        return device(x, y + m.hop, z, c)
    if m.axis == "z":
        return device(x, y, z + m.hop, c)
    return device(x, y, (z // 4) * 4 + (z % 4 + m.hop) % 4, c)


def order_of(plan, tasks, rate=38.0, latency=2.0, late=4.0):
    free, got, sent, events, steps = {}, set(), set(), [(0.0, 0, "g"), (late, 1, "i")], []
    heapq.heapify(events)
    count, now, todo, idle = 2, 0.0, list(tasks), 0.0
    while events or todo:
        ready = next((t for t in todo if all(d in got for d in t[1])), None)
        if ready and not (events and events[0][0] <= now):
            todo.remove(ready)
            steps.append(("task", ready[0]))
            got.add(ready[0])
            now += ready[2]
            continue
        at, _, name = heapq.heappop(events)
        now = max(now, at)
        got.add(name)
        steps.append(("wait", name))
        for m in plan:
            if m.name in sent or not all(d in got for d in m.deps):
                continue
            sent.add(m.name)
            steps.append(("send", m.name))
            if m.axis == "i":
                links, kb = ("z+", "z-"), m.kb
            elif abs(m.hop) > 1:
                links, kb = (m.axis + "+", m.axis + "-"), m.kb
            else:
                links, kb = ((m.axis + "+",) if m.hop > 0 else (m.axis + "-",)), m.kb
            end = max(now, *(free.get(k, 0.0) for k in links)) + kb / rate
            for k in links:
                free[k] = end
            heapq.heappush(events, (end + latency, count, m.name))
            count += 1
    return steps, now


def split(v):
    high = v.astype(BF16)
    return high, (v - high.astype(F32)).astype(BF16)


def dot3(a, b, dims):
    (ah, al), (bh, bl) = a, b
    return (
        lax.dot_general(ah, bh, dims, preferred_element_type=F32)
        + lax.dot_general(ah, bl, dims, preferred_element_type=F32)
        + lax.dot_general(al, bh, dims, preferred_element_type=F32)
    )


RS = ("R1", "L1", "R1b", "L1b", "R2", "L2", "Z")


def kernel(
    li_hbm, og_hbm, pi_hbm, po_hbm, inv_hbm, st_hbm, len_ref, ord_ref, out_ref,
    li, og, pi, po, inv, raw, st_hi, st_lo, pg, pin, rg, rin, grads, ins, q, sc, rsc, fin,
    load_sem, gsend, grecv, rsend, rrecv, ssend, srecv, fsend, frecv,
):
    me = x, y, z, c = place()
    zlo, zhi = z % 4, z // 4
    loads = [
        pltpu.make_async_copy(src, dst, load_sem.at[n])
        for n, (src, dst) in enumerate(
            ((og_hbm, og), (po_hbm, po), (li_hbm, li), (pi_hbm, pi), (inv_hbm, inv), (st_hbm, raw.at[c]))
        )
    ]
    for copy in loads[:5]:
        copy.start()
    line = [device(x, y, zhi * 4 + (zlo + k) % 4, c) for k in (1, 2, 3)]
    partners = [
        device(x + 1, y, z, c), device(x - 1, y, z, c), device(x + 2, y, z, c),
        device(x, y + 1, z, c), device(x, y - 1, z, c), device(x, y + 2, z, c),
        device(x, y, z + 1, c), device(x, y, z - 1, c), device(x, y, z + 4, c),
        device(x, y, z, c + 1), device(x, y, z + 4, c + 1), *line,
    ]
    barrier = pltpu.get_barrier_semaphore()
    for d in partners:
        pl.semaphore_signal(barrier, inc=1, device_id=d, device_id_type=MESH)
    pl.semaphore_wait(barrier, len(partners))

    def remote(src, dst, send, recv, d):
        return pltpu.make_async_remote_copy(src, dst, send, recv, device_id=d, device_id_type=MESH)

    right, left, core = device(x + 1, y, z, c), device(x - 1, y, z, c), device(x, y, z, c + 1)
    xr, xl, xo = (x + 1) % NX, (x - 1) % NX, (x + 2) % NX
    swap = remote(st_hbm, raw.at[c], fsend.at[3], frecv.at[3], core)

    def reduce_plan(n, buf, got):
        def one(k, src, d):
            return remote(src, got.at[k], rsend.at[n, k], rrecv.at[n, k], d)

        return {
            "R1": one(0, buf.at[xo, 0], right), "L1": one(1, buf.at[xo, 1], left),
            "R1b": one(2, buf.at[xr, 1], right), "L1b": one(3, buf.at[xl, 0], left),
            "R2": one(4, buf.at[xr, 0], right), "L2": one(5, buf.at[xl, 1], left),
            "Z": one(6, buf.at[x, 1 - zhi], device(x, y, z + 4, c)),
        }

    first, second = reduce_plan(0, pg, rg), reduce_plan(1, pin, rin)

    loads[0].wait()
    loads[1].wait()
    pg[...] = jnp.dot(og[...], po[...], preferred_element_type=F32).reshape(pg.shape)
    for k in ("R1", "L1", "R1b", "L1b"):
        first[k].start()
    loads[2].wait()
    loads[3].wait()
    pin[...] = lax.dot_general(
        pi[...], li[...], (((0,), (1,)), ((), ())), preferred_element_type=F32
    ).reshape(pin.shape)
    for k in ("R1", "L1", "R1b", "L1b"):
        second[k].start()
    loads[5].start()
    swap.start()

    position = lax.broadcasted_iota(jnp.int32, (8, 512), 1)
    slots, begin = jnp.zeros((8, 512), F32), jnp.int32(0)
    for k in range(QB):
        end = begin + len_ref[0, k]
        here = (position >= begin) & (position < end)
        slots = slots + jnp.where(here, ord_ref[0, k], 0).astype(F32)
        begin = end
    ins[y, zlo, 32:40, :] = slots

    def halfway(cps, buf, got):
        cps["R1"].wait_recv()
        buf[xr, 0] = buf[xr, 0] + got[0]
        cps["R2"].start()
        cps["L1"].wait_recv()
        buf[xl, 1] = buf[xl, 1] + got[1]
        cps["L2"].start()

    def reduced(cps, buf, got):
        for k in ("R1b", "L1b", "R2", "L2"):
            cps[k].wait_recv()
        buf[x, 0] = buf[x, 0] + (got[3] + got[4])
        buf[x, 1] = buf[x, 1] + (got[2] + got[5])
        cps["Z"].start()

    halfway(first, pg, rg)
    halfway(second, pin, rin)
    reduced(first, pg, rg)
    reduced(second, pin, rin)

    plan, needs = gather_plan(me, grads, ins)
    copies = {
        m.name: remote(m.ref, m.ref, gsend.at[n], grecv.at[n], target(me, m)) for n, m in enumerate(plan)
    }

    def prepare(part):
        if part == 0:
            loads[4].wait()
            loads[5].wait()
            swap.wait()

        @pl.loop(part * 4, part * 4 + 4)
        def _(k):
            cols = pl.ds(pl.multiple_of(k * 512, 512), 512)
            for core_of in range(2):
                high, low = split(raw[core_of, :, cols] * inv[:, cols])
                st_hi[core_of, :, cols] = high
                st_lo[core_of, :, cols] = low

    def outer(r, part):
        by = (y + r) % NY
        high_at = NEAR.index(r) * 64 if r != FAR else 384
        low_at = high_at + (192 if r != FAR else 64)

        @pl.loop(part * 2, part * 2 + 2)
        def _(bz):
            g = split(grads[by, bz].reshape(512, 256))
            mine = ins[by, bz]
            rows = mine[0:32, :]
            member = (mine[32:33, :] == lax.broadcasted_iota(jnp.int32, (QB, 512), 0).astype(F32)).astype(F32)
            high = rows.astype(BF16).astype(F32)
            masked = [
                (v[:, None, :] * member[None]).reshape(512, 512).astype(BF16) for v in (high, rows - high)
            ]
            high, low = split(dot3(masked, g, (((1,), (0,)), ((), ()))))
            for i in range(32):
                cols = slice(i * 256, (i + 1) * 256)
                q[pl.ds(pl.multiple_of(high_at + bz * QB, QB), QB), cols] = high[i * QB:(i + 1) * QB]
                q[pl.ds(pl.multiple_of(low_at + bz * QB, QB), QB), cols] = low[i * QB:(i + 1) * QB]

    last = (((1,), (1,)), ((), ()))

    def near_scores(part):
        if part == 0:
            sc[...] = jnp.zeros_like(sc)

        @pl.loop(part * 2, part * 2 + 2)
        def _(k):
            cols = pl.ds(pl.multiple_of(k * 1024, 1024), 1024)
            for core_of in range(2):
                both = lax.dot_general(q[0:384, cols], st_hi[core_of, :, cols], last, preferred_element_type=F32)
                high = lax.dot_general(q[0:192, cols], st_lo[core_of, :, cols], last, preferred_element_type=F32)
                total = both[0:192] + both[192:384] + high
                for n, r in enumerate(NEAR):
                    to = (y + r) % NX
                    sc[to, :, core_of] = sc[to, :, core_of] + total[n * 64:(n + 1) * 64].reshape(2, 32, 192)

    def far_scores():
        def step(k, total):
            cols = pl.ds(pl.multiple_of(k * 1024, 1024), 1024)
            sums = []
            for core_of in range(2):
                both = lax.dot_general(st_hi[core_of, :, cols], q[384:512, cols], last, preferred_element_type=F32)
                high = lax.dot_general(st_lo[core_of, :, cols], q[384:448, cols], last, preferred_element_type=F32)
                sums.append((total[core_of][0] + both, total[core_of][1] + high))
            return tuple(sums)

        zero = (jnp.zeros((192, 128), F32), jnp.zeros((192, 64), F32))
        total = lax.fori_loop(0, 8, step, (zero, zero))
        for core_of in range(2):
            both, high = total[core_of]
            rows = (both[:, 0:64] + both[:, 64:128] + high).T
            sc[(y + FAR) % NX, :, core_of] = rows.reshape(2, 32, 192)

    def pass_on(r):
        to = (y + r) % NX
        slot = (x - to + NX - 1) % NX

        @pl.when(to != x)
        def _():
            remote(sc.at[to], rsc.at[slot], ssend.at[slot], srecv.at[slot], device(to, y, z, c)).start()

    tasks = [(f"prepare{n}", (), 0.6) for n in range(4)]
    run = {f"prepare{n}": (prepare, (n,)) for n in range(4)}
    done = [f"prepare{n}" for n in range(4)]
    for r in NEAR:
        for n in range(2):
            tasks.append((f"outer{r},{n}", tuple(needs[r]), 1.3))
            run[f"outer{r},{n}"] = (outer, (r, n))
            done.append(f"outer{r},{n}")
    for n in range(4):
        tasks.append((f"near{n}", tuple(done), 1.5))
        run[f"near{n}"] = (near_scores, (n,))
        done.append(f"near{n}")
    for r in NEAR:
        tasks.append((f"pass{r}", tuple(done), 0.1))
        run[f"pass{r}"] = (pass_on, (r,))
    for n in range(2):
        tasks.append((f"outer{FAR},{n}", tuple(done) + tuple(needs[FAR]), 1.3))
        run[f"outer{FAR},{n}"] = (outer, (FAR, n))

    for verb, name in order_of(plan, tasks)[0]:
        if name == "g":
            first["Z"].wait_recv()
            grads[y, zlo, x, zhi] = pg[x, zhi] + rg[6]
        elif name == "i":
            second["Z"].wait_recv()
            ins[y, zlo, 0:32, :] = pin[x, zhi] + rin[6]
        elif verb == "send":
            copies[name].start()
        elif verb == "wait":
            copies[name].wait_recv()
        else:
            work, given = run[name]
            work(*given)
    far_scores()
    pass_on(FAR)

    sends = [
        remote(sc.at[x], rsc.at[n], ssend.at[n], srecv.at[n], right) for n in range(3)
    ]
    for copy in sends:
        copy.wait_recv()
    sc[x] = sc[x] + (rsc[0] + rsc[1]) + rsc[2]
    ends = [
        remote(sc.at[x, 1 - zhi, c], fin.at[0], fsend.at[0], frecv.at[0], device(x, y, z + 4, c)),
        remote(sc.at[x, 1 - zhi, 1 - c], fin.at[1], fsend.at[1], frecv.at[1], device(x, y, z + 4, c + 1)),
        remote(sc.at[x, zhi, 1 - c], fin.at[2], fsend.at[2], frecv.at[2], core),
    ]
    for copy in ends:
        copy.start()
    for copy in ends:
        copy.wait_recv()
    mine = sc[x, zhi, c] + fin[0]
    theirs = fin[1] + fin[2]
    for half in range(2):
        part = slice(half * QB, (half + 1) * QB)
        out_ref[pl.ds(pl.multiple_of(half * 32 + c * QB, QB), QB), :] = mine[part]
        out_ref[pl.ds(pl.multiple_of(half * 32 + (1 - c) * QB, QB), QB), :] = theirs[part]

    for copy in (*first.values(), *second.values(), *copies.values(), *sends, *ends):
        copy.wait_send()


def body(layer_input, out_grad, proj_in, proj_out, inv_diag, stored, seq_lengths, query_order):
    hbm, smem = pl.BlockSpec(memory_space=pl.ANY), pl.BlockSpec(memory_space=pltpu.SMEM)
    dma = pltpu.SemaphoreType.DMA
    return pl.pallas_call(
        kernel,
        out_shape=jax.ShapeDtypeStruct((64, 192), F32),
        in_specs=[hbm] * 6 + [smem] * 2,
        out_specs=pl.BlockSpec(memory_space=pltpu.VMEM),
        scratch_shapes=[
            pltpu.VMEM((512, 1024), BF16),
            pltpu.VMEM((512, 1024), BF16),
            pltpu.VMEM((1024, 256), BF16),
            pltpu.VMEM((1024, 256), BF16),
            pltpu.VMEM((1, 8192), F32),
            pltpu.VMEM((2, 192, 8192), F32),
            pltpu.VMEM((2, 192, 8192), BF16),
            pltpu.VMEM((2, 192, 8192), BF16),
            pltpu.VMEM((4, 2, 64, 256), F32),
            pltpu.VMEM((4, 2, 32, 512), F32),
            pltpu.VMEM((7, 64, 256), F32),
            pltpu.VMEM((7, 32, 512), F32),
            pltpu.VMEM((4, 4, 4, 2, TOK, 256), F32),
            pltpu.VMEM((4, 4, INROWS, 512), F32),
            pltpu.VMEM((512, 8192), BF16),
            pltpu.VMEM((4, 2, 2, 32, 192), F32),
            pltpu.VMEM((3, 2, 2, 32, 192), F32),
            pltpu.VMEM((3, 32, 192), F32),
            dma((6,)),
            dma((160,)), dma((160,)),
            dma((2, 7)), dma((2, 7)),
            dma((3,)), dma((3,)),
            dma((4,)), dma((4,)),
        ],
        compiler_params=pltpu.CompilerParams(
            collective_id=0, has_side_effects=True, vmem_limit_bytes=60 * 2**20
        ),
    )(layer_input, out_grad, proj_in, proj_out, inv_diag.reshape(1, -1), stored, seq_lengths, query_order)


def solution(mesh):
    return jax.shard_map(
        body,
        mesh=mesh,
        in_specs=(
            P("store", "feat"),
            P("store", "feat"),
            P("feat", None),
            P("feat", None),
            P("feat"),
            P("store", "feat"),
            P("store", None),
            P("store", None),
        ),
        out_specs=P("feat", "store"),
        check_vma=False,
    )
```

```python
import heapq

import jax
import jax.numpy as jnp
from jax import lax
from jax.experimental import pallas as pl
from jax.experimental.pallas import tpu as pltpu
from jax.sharding import PartitionSpec as P

MESH = pl.DeviceIdType.MESH
F32, BF16 = jnp.float32, jnp.bfloat16
NX, NY, NZ = 4, 4, 8
QB = 16
A0, B0, C0, TOK = 0, 16, 40, 64
INROWS = 136


def place():
    f, s = lax.axis_index("feat"), lax.axis_index("store")
    return f // 2, s // 8, (f % 2) * 4 + (s // 2) % 4, s % 2


def device(x, y, z, c):
    x, y, z, c = x % NX, y % NY, z % NZ, c % 2
    return (x * 2 + z // 4, y * 8 + (z % 4) * 2 + c)


class Message:
    def __init__(self, name, deps, kb, axis, hop, ref):
        self.name, self.deps, self.kb, self.axis, self.hop, self.ref = name, tuple(deps), kb, axis, hop, ref


def ring(k, sign, tag):
    return f"{tag}{sign * k}"


def around(tag):
    return [ring(k, s, tag) for k in (1, 2, 3, 4) for s in (1, -1)]


NEAR, FAR = (0, 1, -1), 2


def gather_plan(me, grads, ins):
    x, y, z, c = me
    out = []

    def zz(v):
        return v % 4, (v % NZ) // 4

    def add(name, deps, kb, axis, hop, ref):
        out.append(Message(name, deps, kb, axis, hop, ref))

    def ga(zv, yv, xs=slice(None)):
        lo, hi = zz(zv)
        return grads.at[yv % NY, lo, xs, hi, A0:B0, :]

    def gb(zv, yv, xv):
        lo, hi = zz(zv)
        return grads.at[yv % NY, lo, xv % NX, hi, B0:C0, :]

    def gz(xv, yv, rows, zs=slice(None)):
        return grads.at[yv % NY, zs, xv % NX, :, rows, :]

    first, second = pl.ds(0, 2), pl.ds(2, 2)
    brows, crows = slice(B0, C0), slice(C0, TOK)
    ka, kb, kc = (B0 - A0), (C0 - B0), (TOK - C0)
    lo, hi = zz(z)
    from_y = {1: -1, -1: 1, 2: 2}
    for k in (1, 2, 3, 4):
        for sign in (1, -1):
            zlo, zhi = zz(z - sign * (k - 1))
            cols = slice(None) if k < 4 else pl.ds(0 if sign > 0 else 128, 128)
            deps = ["g"] if k == 1 else [ring(k - 1, sign, "Cz")]
            add(ring(k, sign, "Cz"), deps, kc if k < 4 else kc / 2, "z", sign, grads.at[y, zlo, x, zhi, crows, cols])
    call = ["g"] + around("Cz")
    for hop in (1, -1, 2):
        add(f"Ax{hop}", ["g"], ka, "x", hop, grads.at[y, lo, x, hi, A0:B0, :])
    aall = ["g"] + [f"Ax{h}" for h in (1, -1, 2)]
    for hop in (1, -1, 2):
        add(f"By{hop}", ["g"], kb, "y", hop, gb(z, y, x))
    for hop in (1, -1, 2):
        add(f"Ay{hop}", aall, 4 * ka, "y", hop, ga(z, y))
    for sign in (1, -1):
        add(f"Cx{sign}", call, 8 * kc, "x", sign, gz(x, y, crows))
    for sign in (1, -1):
        half = first if sign > 0 else second
        add(f"Cx{2 * sign}", [f"Cx{sign}"], 4 * kc, "x", sign, gz(x - sign, y, crows, half))
    for k in (1, 2, 3):
        add(f"Iz{k}", ["i", "Cz3", "Cz-3"], 68, "i", k, ins.at[y, lo])
    iall = ["i"] + [f"Iz{k}" for k in (1, 2, 3)]
    needs = {}
    across = {s: [f"C0y{s},{d}" for d in (0, -1, 1, -2, 2, -3, 3, 4)] for s in (1, -1)}
    for r in (*NEAR, FAR):
        tag = f"B{r}z"
        here = ["g"] if r == 0 else [f"By{from_y[r]}"]
        held = ["A0z1", "A0z-1"] if r == FAR else []
        for k in (1, 2, 3, 4):
            for sign in (1, -1):
                deps = here + held if k == 1 else [ring(k - 1, sign, tag)]
                zv = z - sign * (k - 1)
                ref = gb(zv, y + r, x)
                if k == 4:
                    zlo, zhi = zz(zv)
                    ref = grads.at[(y + r) % NY, zlo, x, zhi, brows, pl.ds(0 if sign > 0 else 128, 128)]
                add(ring(k, sign, tag), deps, kb if k < 4 else kb / 2, "z", sign, ref)
        ball = here + around(tag)
        brought = []
        if r == 0:
            for d in (0, -1, 1, -2, 2, -3, 3, 4):
                deps = ["g"] if d == 0 else ([ring(4, 1, tag), ring(4, -1, tag)] if d == 4 else [f"{tag}{-d}"])
                for sign in (1, -1):
                    add(f"B0x{sign},{d}", deps, kb, "x", sign, gb(z + d, y, x))
            came = {s: [f"B0x{s},{d}" for d in (0, -1, 1, -2, 2, -3, 3, 4)] for s in (1, -1)}
        else:
            for sign in (1, -1):
                add(f"B{r}x{sign}", ball + (["B1x1", "B1x-1"] if r == FAR else []), 8 * kb, "x", sign, gz(x, y + r, brows))
            came = {s: [f"B{r}x{s}"] for s in (1, -1)}
        for sign in (1, -1):
            half = first if sign > 0 else second
            add(f"B{r}x{2 * sign}", came[sign], 4 * kb, "x", sign, gz(x - sign, y + r, brows, half))
            brought += came[sign] + [f"B{r}x{2 * sign}"]
        tag = f"A{r}z"
        here = aall if r == 0 else [f"Ay{from_y[r]}"]
        held = ["A1z3", "A-1z3"] if r == FAR else ["B1z3", "B1z-3"]
        for k in (1, 2, 3, 4):
            for sign in (1, -1):
                deps = here + held if k == 1 else [ring(k - 1, sign, tag)]
                xs = slice(None) if k < 4 else (first if sign > 0 else second)
                ref = ga(z - sign * (k - 1), y + r, xs)
                add(ring(k, sign, tag), deps, 4 * ka if k < 4 else 2 * ka, "z", sign, ref)
        needs[r] = ball + brought + here + around(tag)
        if r == 0:
            needs[r] += call + ["Cx1", "Cx-1", "Cx2", "Cx-2"] + iall
            for d in (0, -1, 1, -2, 2, -3, 3, 4):
                deps = ["g"] if d == 0 else (["Cz4", "Cz-4"] if d == 4 else [f"Cz{-d}"])
                zlo, zhi = zz(z + d)
                for sign in (1, -1):
                    add(f"C0y{sign},{d}", deps, kc, "y", sign, grads.at[y, zlo, x, zhi, crows, :])
            for d in (-1, 1, 2):
                deps = ["Cx2", "Cx-2"] if d == 2 else [f"Cx{-d}"]
                for sign in (1, -1):
                    add(f"C{d}y{sign}", deps, 8 * kc, "y", sign, gz(x + d, y, crows))
            for sign in (1, -1):
                add(f"Iy{sign}", iall, 272, "y", sign, ins.at[y])
        elif r != FAR:
            sign = from_y[r]
            needs[r] += [f"C{d}y{sign}" for d in (-1, 1, 2)] + across[sign] + [f"Iy{sign}"]
        else:
            for sign in (1, -1):
                half = first if sign > 0 else second
                add(f"Iy{2 * sign}", [f"Iy{sign}", f"C2y{sign}"], 136, "y", sign, ins.at[(y - sign) % NY, half])
                needs[r] += [f"Iy{2 * sign}"]
            for d in (0, -1, 1, 2):
                for sign in (1, -1):
                    half = first if sign > 0 else second
                    deps = (across[sign] if d == 0 else [f"C{d}y{sign}"]) + [f"C1y{sign}"]
                    add(f"C{d}y{2 * sign}", deps, 4 * kc, "y", sign, gz(x + d, y - sign, crows, half))
                    needs[r] += [f"C{d}y{2 * sign}"]
    return out, needs


def target(me, m):
    x, y, z, c = me
    if m.axis == "x":
        return device(x + m.hop, y, z, c)
    if m.axis == "y":
        return device(x, y + m.hop, z, c)
    if m.axis == "z":
        return device(x, y, z + m.hop, c)
    return device(x, y, (z // 4) * 4 + (z % 4 + m.hop) % 4, c)


def order_of(plan, tasks, rate=38.0, latency=2.0, late=4.0):
    free, got, sent, events, steps = {}, set(), set(), [(0.0, 0, "g"), (late, 1, "i")], []
    heapq.heapify(events)
    count, now, todo, idle = 2, 0.0, list(tasks), 0.0
    while events or todo:
        ready = next((t for t in todo if all(d in got for d in t[1])), None)
        if ready and not (events and events[0][0] <= now):
            todo.remove(ready)
            steps.append(("task", ready[0]))
            got.add(ready[0])
            now += ready[2]
            continue
        at, _, name = heapq.heappop(events)
        now = max(now, at)
        got.add(name)
        steps.append(("wait", name))
        for m in plan:
            if m.name in sent or not all(d in got for d in m.deps):
                continue
            sent.add(m.name)
            steps.append(("send", m.name))
            if m.axis == "i":
                links, kb = ("z+", "z-"), m.kb
            elif abs(m.hop) > 1:
                links, kb = (m.axis + "+", m.axis + "-"), m.kb
            else:
                links, kb = ((m.axis + "+",) if m.hop > 0 else (m.axis + "-",)), m.kb
            end = max(now, *(free.get(k, 0.0) for k in links)) + kb / rate
            for k in links:
                free[k] = end
            heapq.heappush(events, (end + latency, count, m.name))
            count += 1
    return steps, now


def split(v):
    high = v.astype(BF16)
    return high, (v - high.astype(F32)).astype(BF16)


def dot3(a, b, dims):
    (ah, al), (bh, bl) = a, b
    return (
        lax.dot_general(ah, bh, dims, preferred_element_type=F32)
        + lax.dot_general(ah, bl, dims, preferred_element_type=F32)
        + lax.dot_general(al, bh, dims, preferred_element_type=F32)
    )


RS = ("R1", "L1", "R1b", "L1b", "R2", "L2", "Z")


def kernel(
    li_hbm, og_hbm, pi_hbm, po_hbm, inv_hbm, st_hbm, len_ref, ord_ref, out_ref,
    li, og, pi, po, inv, raw, st_hi, st_lo, pg, pin, rg, rin, grads, ins, q, sc, rsc, fin,
    load_sem, gsend, grecv, rsend, rrecv, ssend, srecv, fsend, frecv,
):
    me = x, y, z, c = place()
    zlo, zhi = z % 4, z // 4
    rows_of = pl.ds(pl.multiple_of(c * 192, 192), 192)
    loads = [
        pltpu.make_async_copy(src, dst, load_sem.at[n])
        for n, (src, dst) in enumerate(
            ((og_hbm, og), (po_hbm, po), (li_hbm, li), (pi_hbm, pi), (inv_hbm, inv), (st_hbm, raw.at[rows_of]))
        )
    ]
    for copy in loads[:5]:
        copy.start()
    line = [device(x, y, zhi * 4 + (zlo + k) % 4, c) for k in (1, 2, 3)]
    partners = [
        device(x + 1, y, z, c), device(x - 1, y, z, c), device(x + 2, y, z, c),
        device(x, y + 1, z, c), device(x, y - 1, z, c), device(x, y + 2, z, c),
        device(x, y, z + 1, c), device(x, y, z - 1, c), device(x, y, z + 4, c),
        device(x, y, z, c + 1), device(x, y, z + 4, c + 1), *line,
    ]
    barrier = pltpu.get_barrier_semaphore()
    for d in partners:
        pl.semaphore_signal(barrier, inc=1, device_id=d, device_id_type=MESH)

    def remote(src, dst, send, recv, d):
        return pltpu.make_async_remote_copy(src, dst, send, recv, device_id=d, device_id_type=MESH)

    right, left, core = device(x + 1, y, z, c), device(x - 1, y, z, c), device(x, y, z, c + 1)
    xr, xl, xo = (x + 1) % NX, (x - 1) % NX, (x + 2) % NX
    swap = remote(st_hbm, raw.at[rows_of], fsend.at[3], frecv.at[3], core)

    def reduce_plan(n, buf, got):
        def one(k, src, d):
            return remote(src, got.at[k], rsend.at[n, k], rrecv.at[n, k], d)

        return {
            "R1": one(0, buf.at[xo, 0], right), "L1": one(1, buf.at[xo, 1], left),
            "R1b": one(2, buf.at[xr, 1], right), "L1b": one(3, buf.at[xl, 0], left),
            "R2": one(4, buf.at[xr, 0], right), "L2": one(5, buf.at[xl, 1], left),
            "Z": one(6, buf.at[x, 1 - zhi], device(x, y, z + 4, c)),
        }

    first, second = reduce_plan(0, pg, rg), reduce_plan(1, pin, rin)

    loads[0].wait()
    loads[1].wait()
    pg[...] = jnp.dot(og[...], po[...], preferred_element_type=F32).reshape(pg.shape)
    pl.semaphore_wait(barrier, len(partners))
    for k in ("R1", "L1", "R1b", "L1b"):
        first[k].start()
    loads[2].wait()
    loads[3].wait()
    pin[...] = lax.dot_general(
        pi[...], li[...], (((0,), (1,)), ((), ())), preferred_element_type=F32
    ).reshape(pin.shape)
    for k in ("R1", "L1", "R1b", "L1b"):
        second[k].start()
    loads[5].start()
    swap.start()

    position = lax.broadcasted_iota(jnp.int32, (8, 128), 0) * 128 + lax.broadcasted_iota(jnp.int32, (8, 128), 1)
    slots, begin = jnp.zeros((8, 128), F32), jnp.int32(0)
    for k in range(QB):
        end = begin + len_ref[0, k]
        here = (position >= begin) & (position < end)
        slots = slots + jnp.where(here, ord_ref[0, k], 0).astype(F32)
        begin = end
    ins[y, zlo, 128:136, :] = slots

    def halfway(cps, buf, got):
        cps["R1"].wait_recv()
        buf[xr, 0] = buf[xr, 0] + got[0]
        cps["R2"].start()
        cps["L1"].wait_recv()
        buf[xl, 1] = buf[xl, 1] + got[1]
        cps["L2"].start()

    def reduced(cps, buf, got):
        for k in ("R1b", "L1b", "R2", "L2"):
            cps[k].wait_recv()
        buf[x, 0] = buf[x, 0] + (got[3] + got[4])
        buf[x, 1] = buf[x, 1] + (got[2] + got[5])
        cps["Z"].start()

    halfway(first, pg, rg)
    halfway(second, pin, rin)
    reduced(first, pg, rg)
    reduced(second, pin, rin)

    plan, needs = gather_plan(me, grads, ins)
    copies = {
        m.name: remote(m.ref, m.ref, gsend.at[n], grecv.at[n], target(me, m)) for n, m in enumerate(plan)
    }

    def prepare(part):
        if part == 0:
            loads[4].wait()
            loads[5].wait()
            swap.wait()

        @pl.loop(part * 4, part * 4 + 4)
        def _(k):
            cols = pl.ds(pl.multiple_of(k * 512, 512), 512)
            high, low = split(raw[:, cols] * inv[:, cols])
            st_hi[:, cols] = high
            st_lo[:, cols] = low

    def outer(r, part):
        by = (y + r) % NY
        high_at = NEAR.index(r) * 64 if r != FAR else 384
        low_at = high_at + (192 if r != FAR else 64)

        @pl.loop(part * 2, part * 2 + 2)
        def _(bz):
            g = split(grads[by, bz].reshape(512, 256))
            mine = ins[by, bz]
            rows = jnp.concatenate([mine[32 * k:32 * k + 32] for k in range(4)], axis=1)
            slot = jnp.concatenate([mine[128 + k:129 + k] for k in range(4)], axis=1)
            member = (slot == lax.broadcasted_iota(jnp.int32, (QB, 512), 0).astype(F32)).astype(F32)
            high = rows.astype(BF16).astype(F32)
            masked = [
                (v[:, None, :] * member[None]).reshape(512, 512).astype(BF16) for v in (high, rows - high)
            ]
            high, low = split(dot3(masked, g, (((1,), (0,)), ((), ()))))
            for i in range(32):
                cols = slice(i * 256, (i + 1) * 256)
                q[pl.ds(pl.multiple_of(high_at + bz * QB, QB), QB), cols] = high[i * QB:(i + 1) * QB]
                q[pl.ds(pl.multiple_of(low_at + bz * QB, QB), QB), cols] = low[i * QB:(i + 1) * QB]

    last = (((1,), (1,)), ((), ()))

    def near_scores(part):
        if part == 0:
            sc[...] = jnp.zeros_like(sc)

        @pl.loop(part * 2, part * 2 + 2)
        def _(k):
            cols = pl.ds(pl.multiple_of(k * 1024, 1024), 1024)
            both = lax.dot_general(q[0:384, cols], st_hi[:, cols], last, preferred_element_type=F32)
            high = lax.dot_general(q[0:192, cols], st_lo[:, cols], last, preferred_element_type=F32)
            total = both[0:192] + both[192:384] + high
            for n, r in enumerate(NEAR):
                to = (y + r) % NX
                sc[to] = sc[to] + total[n * 64:(n + 1) * 64].reshape(2, 32, 384)

    def far_scores():
        def step(k, total):
            cols = pl.ds(pl.multiple_of(k * 1024, 1024), 1024)
            both = lax.dot_general(st_hi[:, cols], q[384:512, cols], last, preferred_element_type=F32)
            high = lax.dot_general(st_lo[:, cols], q[384:448, cols], last, preferred_element_type=F32)
            return total[0] + both, total[1] + high

        both, high = lax.fori_loop(0, 8, step, (jnp.zeros((384, 128), F32), jnp.zeros((384, 64), F32)))
        rows = (both[:, 0:64] + both[:, 64:128] + high).T
        sc[(y + FAR) % NX] = rows.reshape(2, 32, 384)

    def pass_on(r):
        to = (y + r) % NX
        slot = (x - to + NX - 1) % NX

        @pl.when(to != x)
        def _():
            remote(sc.at[to], rsc.at[slot], ssend.at[slot], srecv.at[slot], device(to, y, z, c)).start()

    tasks = [(f"prepare{n}", (), 0.6) for n in range(4)]
    run = {f"prepare{n}": (prepare, (n,)) for n in range(4)}
    done = [f"prepare{n}" for n in range(4)]
    for r in NEAR:
        for n in range(2):
            tasks.append((f"outer{r},{n}", tuple(needs[r]), 1.3))
            run[f"outer{r},{n}"] = (outer, (r, n))
            done.append(f"outer{r},{n}")
    for n in range(4):
        tasks.append((f"near{n}", tuple(done), 1.5))
        run[f"near{n}"] = (near_scores, (n,))
        done.append(f"near{n}")
    for r in NEAR:
        tasks.append((f"pass{r}", tuple(done), 0.1))
        run[f"pass{r}"] = (pass_on, (r,))
    for n in range(2):
        tasks.append((f"outer{FAR},{n}", tuple(done) + tuple(needs[FAR]), 1.3))
        run[f"outer{FAR},{n}"] = (outer, (FAR, n))

    for verb, name in order_of(plan, tasks)[0]:
        if name == "g":
            first["Z"].wait_recv()
            grads[y, zlo, x, zhi] = pg[x, zhi] + rg[6]
        elif name == "i":
            second["Z"].wait_recv()
            whole = pin[x, zhi] + rin[6]
            for k in range(4):
                ins[y, zlo, 32 * k:32 * k + 32, :] = whole[:, 128 * k:128 * k + 128]
        elif verb == "send":
            copies[name].start()
        elif verb == "wait":
            copies[name].wait_recv()
        else:
            work, given = run[name]
            work(*given)
    far_scores()
    pass_on(FAR)

    sends = [
        remote(sc.at[x], rsc.at[n], ssend.at[n], srecv.at[n], right) for n in range(3)
    ]
    for copy in sends:
        copy.wait_recv()
    sc[x] = sc[x] + (rsc[0] + rsc[1]) + rsc[2]
    ours, others = (pl.ds(pl.multiple_of(k * 128, 128), 256) for k in (c, 1 - c))
    ends = [
        remote(sc.at[x, 1 - zhi, :, ours], fin.at[0], fsend.at[0], frecv.at[0], device(x, y, z + 4, c)),
        remote(sc.at[x, 1 - zhi, :, others], fin.at[1], fsend.at[1], frecv.at[1], device(x, y, z + 4, c + 1)),
        remote(sc.at[x, zhi, :, others], fin.at[2], fsend.at[2], frecv.at[2], core),
    ]
    for copy in ends:
        copy.start()
    for copy in ends:
        copy.wait_recv()
    mine, theirs = (
        jnp.where(c == 0, v[:, 0:192], v[:, 64:256])
        for v in (sc[x, zhi, :, ours] + fin[0], fin[1] + fin[2])
    )
    for half in range(2):
        part = slice(half * QB, (half + 1) * QB)
        out_ref[pl.ds(pl.multiple_of(half * 32 + c * QB, QB), QB), :] = mine[part]
        out_ref[pl.ds(pl.multiple_of(half * 32 + (1 - c) * QB, QB), QB), :] = theirs[part]

    for copy in (*first.values(), *second.values(), *copies.values(), *sends, *ends):
        copy.wait_send()


def body(layer_input, out_grad, proj_in, proj_out, inv_diag, stored, seq_lengths, query_order):
    hbm, smem = pl.BlockSpec(memory_space=pl.ANY), pl.BlockSpec(memory_space=pltpu.SMEM)
    dma = pltpu.SemaphoreType.DMA
    return pl.pallas_call(
        kernel,
        out_shape=jax.ShapeDtypeStruct((64, 192), F32),
        in_specs=[hbm] * 6 + [smem] * 2,
        out_specs=pl.BlockSpec(memory_space=pltpu.VMEM),
        scratch_shapes=[
            pltpu.VMEM((512, 1024), BF16),
            pltpu.VMEM((512, 1024), BF16),
            pltpu.VMEM((1024, 256), BF16),
            pltpu.VMEM((1024, 256), BF16),
            pltpu.VMEM((1, 8192), F32),
            pltpu.VMEM((384, 8192), F32),
            pltpu.VMEM((384, 8192), BF16),
            pltpu.VMEM((384, 8192), BF16),
            pltpu.VMEM((4, 2, 64, 256), F32),
            pltpu.VMEM((4, 2, 32, 512), F32),
            pltpu.VMEM((7, 64, 256), F32),
            pltpu.VMEM((7, 32, 512), F32),
            pltpu.VMEM((4, 4, 4, 2, TOK, 256), F32),
            pltpu.VMEM((4, 4, INROWS, 128), F32),
            pltpu.VMEM((512, 8192), BF16),
            pltpu.VMEM((4, 2, 32, 384), F32),
            pltpu.VMEM((3, 2, 32, 384), F32),
            pltpu.VMEM((3, 32, 256), F32),
            dma((6,)),
            dma((160,)), dma((160,)),
            dma((2, 7)), dma((2, 7)),
            dma((3,)), dma((3,)),
            dma((4,)), dma((4,)),
        ],
        compiler_params=pltpu.CompilerParams(
            collective_id=0, has_side_effects=True, vmem_limit_bytes=60 * 2**20
        ),
    )(layer_input, out_grad, proj_in, proj_out, inv_diag.reshape(1, -1), stored, seq_lengths, query_order)


def solution(mesh):
    return jax.shard_map(
        body,
        mesh=mesh,
        in_specs=(
            P("store", "feat"),
            P("store", "feat"),
            P("feat", None),
            P("feat", None),
            P("feat"),
            P("store", "feat"),
            P("store", None),
            P("store", None),
        ),
        out_specs=P("feat", "store"),
        check_vma=False,
    )
```

```python
import heapq

import jax
import jax.numpy as jnp
from jax import lax
from jax.experimental import pallas as pl
from jax.experimental.pallas import tpu as pltpu
from jax.sharding import PartitionSpec as P

MESH = pl.DeviceIdType.MESH
F32, BF16 = jnp.float32, jnp.bfloat16
NX, NY, NZ = 4, 4, 8
QB = 16
A0, B0, C0, TOK = 0, 16, 40, 64
INROWS = 136


def place():
    f, s = lax.axis_index("feat"), lax.axis_index("store")
    return f // 2, s // 8, (f % 2) * 4 + (s // 2) % 4, s % 2


def device(x, y, z, c):
    x, y, z, c = x % NX, y % NY, z % NZ, c % 2
    return (x * 2 + z // 4, y * 8 + (z % 4) * 2 + c)


class Message:
    def __init__(self, name, deps, kb, axis, hop, ref):
        self.name, self.deps, self.kb, self.axis, self.hop, self.ref = name, tuple(deps), kb, axis, hop, ref


def ring(k, sign, tag):
    return f"{tag}{sign * k}"


def around(tag):
    return [ring(k, s, tag) for k in (1, 2, 3, 4) for s in (1, -1)]


NEAR, FAR = (0, 1, -1), 2


def gather_plan(me, grads, ins):
    x, y, z, c = me
    out = []

    def zz(v):
        return v % 4, (v % NZ) // 4

    def add(name, deps, kb, axis, hop, ref):
        out.append(Message(name, deps, kb, axis, hop, ref))

    def ga(zv, yv, xs=slice(None)):
        lo, hi = zz(zv)
        return grads.at[yv % NY, lo, xs, hi, A0:B0, :]

    def gb(zv, yv, xv):
        lo, hi = zz(zv)
        return grads.at[yv % NY, lo, xv % NX, hi, B0:C0, :]

    def gz(xv, yv, rows, zs=slice(None)):
        return grads.at[yv % NY, zs, xv % NX, :, rows, :]

    first, second = pl.ds(0, 2), pl.ds(2, 2)
    brows, crows = slice(B0, C0), slice(C0, TOK)
    ka, kb, kc = (B0 - A0), (C0 - B0), (TOK - C0)
    lo, hi = zz(z)
    from_y = {1: -1, -1: 1, 2: 2}
    for k in (1, 2, 3, 4):
        for sign in (1, -1):
            zlo, zhi = zz(z - sign * (k - 1))
            cols = slice(None) if k < 4 else pl.ds(0 if sign > 0 else 128, 128)
            deps = ["gc"] if k == 1 else [ring(k - 1, sign, "Cz")]
            add(ring(k, sign, "Cz"), deps, kc if k < 4 else kc / 2, "z", sign, grads.at[y, zlo, x, zhi, crows, cols])
    call = ["gc"] + around("Cz")
    for hop in (1, -1, 2):
        add(f"Ax{hop}", ["g"], ka, "x", hop, grads.at[y, lo, x, hi, A0:B0, :])
    aall = ["g"] + [f"Ax{h}" for h in (1, -1, 2)]
    for hop in (1, -1, 2):
        add(f"By{hop}", ["g"], kb, "y", hop, gb(z, y, x))
    for hop in (1, -1, 2):
        add(f"Ay{hop}", aall, 4 * ka, "y", hop, ga(z, y))
    crossed = {s: [f"Cx{s},{d}" for d in (0, -1, 1, -2, 2, -3, 3, 4)] for s in (1, -1)}
    for d in (0, -1, 1, -2, 2, -3, 3, 4):
        deps = ["gc"] if d == 0 else (["Cz4", "Cz-4"] if d == 4 else [f"Cz{-d}"])
        zlo, zhi = zz(z + d)
        for sign in (1, -1):
            add(f"Cx{sign},{d}", deps, kc, "x", sign, grads.at[y, zlo, x, zhi, crows, :])
    for sign in (1, -1):
        half = first if sign > 0 else second
        add(f"Cx{2 * sign}", crossed[sign], 4 * kc, "x", sign, gz(x - sign, y, crows, half))
    for k in (1, 2, 3):
        add(f"Iz{k}", ["i", "Cz3", "Cz-3"], 68, "i", k, ins.at[y, lo])
    iall = ["i"] + [f"Iz{k}" for k in (1, 2, 3)]
    needs = {}
    across = {s: [f"C0y{s},{d}" for d in (0, -1, 1, -2, 2, -3, 3, 4)] for s in (1, -1)}
    for r in (*NEAR, FAR):
        tag = f"B{r}z"
        here = ["g"] if r == 0 else [f"By{from_y[r]}"]
        held = ["B0z3", "B0z-3"] if r == FAR else []
        for k in (1, 2, 3, 4):
            for sign in (1, -1):
                deps = here + held if k == 1 else [ring(k - 1, sign, tag)]
                zv = z - sign * (k - 1)
                ref = gb(zv, y + r, x)
                if k == 4:
                    zlo, zhi = zz(zv)
                    ref = grads.at[(y + r) % NY, zlo, x, zhi, brows, pl.ds(0 if sign > 0 else 128, 128)]
                add(ring(k, sign, tag), deps, kb if k < 4 else kb / 2, "z", sign, ref)
        ball = here + around(tag)
        brought = []
        if r == 0:
            for d in (0, -1, 1, -2, 2, -3, 3, 4):
                deps = ["g"] if d == 0 else ([ring(4, 1, tag), ring(4, -1, tag)] if d == 4 else [f"{tag}{-d}"])
                for sign in (1, -1):
                    add(f"B0x{sign},{d}", deps, kb, "x", sign, gb(z + d, y, x))
            came = {s: [f"B0x{s},{d}" for d in (0, -1, 1, -2, 2, -3, 3, 4)] for s in (1, -1)}
        else:
            for sign in (1, -1):
                add(f"B{r}x{sign}", ball + (["B1x1", "B1x-1"] if r == FAR else []), 8 * kb, "x", sign, gz(x, y + r, brows))
            came = {s: [f"B{r}x{s}"] for s in (1, -1)}
        for sign in (1, -1):
            half = first if sign > 0 else second
            add(f"B{r}x{2 * sign}", came[sign], 4 * kb, "x", sign, gz(x - sign, y + r, brows, half))
            brought += came[sign] + [f"B{r}x{2 * sign}"]
        tag = f"A{r}z"
        here = aall if r == 0 else [f"Ay{from_y[r]}"]
        held = ["A0z3", "A0z-3"] if r == FAR else ["B1z3", "B1z-3"]
        for k in (1, 2, 3, 4):
            for sign in (1, -1):
                deps = here + held if k == 1 else [ring(k - 1, sign, tag)]
                xs = slice(None) if k < 4 else (first if sign > 0 else second)
                ref = ga(z - sign * (k - 1), y + r, xs)
                add(ring(k, sign, tag), deps, 4 * ka if k < 4 else 2 * ka, "z", sign, ref)
        needs[r] = ball + brought + here + around(tag)
        if r == 0:
            needs[r] += call + crossed[1] + crossed[-1] + ["Cx2", "Cx-2"] + iall
            for d in (0, -1, 1, -2, 2, -3, 3, 4):
                deps = ["gc"] if d == 0 else (["Cz4", "Cz-4"] if d == 4 else [f"Cz{-d}"])
                zlo, zhi = zz(z + d)
                for sign in (1, -1):
                    add(f"C0y{sign},{d}", deps, kc, "y", sign, grads.at[y, zlo, x, zhi, crows, :])
            for d in (-1, 1, 2):
                deps = ["Cx2", "Cx-2"] if d == 2 else crossed[-d]
                for sign in (1, -1):
                    add(f"C{d}y{sign}", deps, 8 * kc, "y", sign, gz(x + d, y, crows))
            for sign in (1, -1):
                add(f"Iy{sign}", iall, 272, "y", sign, ins.at[y])
        elif r != FAR:
            sign = from_y[r]
            needs[r] += [f"C{d}y{sign}" for d in (-1, 1, 2)] + across[sign] + [f"Iy{sign}"]
        else:
            for sign in (1, -1):
                half = first if sign > 0 else second
                add(f"Iy{2 * sign}", [f"Iy{sign}", f"C2y{sign}"], 136, "y", sign, ins.at[(y - sign) % NY, half])
                needs[r] += [f"Iy{2 * sign}"]
            for sign in (1, -1):
                half = first if sign > 0 else second
                add(f"C2x{sign}", [f"C{-sign}y{2 * sign}"], 4 * kc, "x", sign, gz(x - sign, y + FAR, crows, half))
                needs[r] += [f"C2x{sign}"]
            for d in (-1, 1, 0):
                for sign in (1, -1):
                    half = first if sign > 0 else second
                    deps = (across[sign] if d == 0 else [f"C{d}y{sign}"]) + [f"C1y{sign}"]
                    add(f"C{d}y{2 * sign}", deps, 4 * kc, "y", sign, gz(x + d, y - sign, crows, half))
                    needs[r] += [f"C{d}y{2 * sign}"]
    return out, needs


def target(me, m):
    x, y, z, c = me
    if m.axis == "x":
        return device(x + m.hop, y, z, c)
    if m.axis == "y":
        return device(x, y + m.hop, z, c)
    if m.axis == "z":
        return device(x, y, z + m.hop, c)
    return device(x, y, (z // 4) * 4 + (z % 4 + m.hop) % 4, c)


def order_of(plan, tasks, rate=38.0, latency=2.0, late=5.0):
    free, got, sent, events, steps = {}, set(), set(), [(0.0, 0, "gc"), (1.2, 1, "g"), (late, 2, "i")], []
    heapq.heapify(events)
    count, now, todo = 3, 0.0, list(tasks)
    while events or todo:
        ready = next((t for t in todo if all(d in got for d in t[1])), None)
        if ready and not (events and events[0][0] <= now):
            todo.remove(ready)
            steps.append(("task", ready[0]))
            got.add(ready[0])
            now += ready[2]
            continue
        at, _, name = heapq.heappop(events)
        now = max(now, at)
        got.add(name)
        steps.append(("wait", name))
        for m in plan:
            if m.name in sent or not all(d in got for d in m.deps):
                continue
            sent.add(m.name)
            steps.append(("send", m.name))
            if m.axis == "i":
                links, kb = ("z+", "z-"), m.kb
            elif abs(m.hop) > 1:
                links, kb = (m.axis + "+", m.axis + "-"), m.kb
            else:
                links, kb = ((m.axis + "+",) if m.hop > 0 else (m.axis + "-",)), m.kb
            end = max(now, *(free.get(k, 0.0) for k in links)) + kb / rate
            for k in links:
                free[k] = end
            heapq.heappush(events, (end + latency, count, m.name))
            count += 1
    return steps, now


def split(v):
    high = v.astype(BF16)
    return high, (v - high.astype(F32)).astype(BF16)


def dot3(a, b, dims):
    (ah, al), (bh, bl) = a, b
    return (
        lax.dot_general(ah, bh, dims, preferred_element_type=F32)
        + lax.dot_general(ah, bl, dims, preferred_element_type=F32)
        + lax.dot_general(al, bh, dims, preferred_element_type=F32)
    )


def kernel(
    li_hbm, og_hbm, pi_hbm, po_hbm, inv_hbm, st_hbm, len_ref, ord_ref, out_ref,
    li, og, pi, po, inv, raw, st_hi, st_lo, pg, pin, rg, rin, grads, ins, q, sc, rsc, fin,
    load_sem, gsend, grecv, rsend, rrecv, ssend, srecv, fsend, frecv,
):
    me = x, y, z, c = place()
    zlo, zhi = z % 4, z // 4
    rows_of = pl.ds(pl.multiple_of(c * 192, 192), 192)
    loads = [
        pltpu.make_async_copy(src, dst, load_sem.at[n])
        for n, (src, dst) in enumerate(
            ((og_hbm, og), (po_hbm, po), (li_hbm, li), (pi_hbm, pi), (inv_hbm, inv), (st_hbm, raw.at[rows_of]))
        )
    ]
    for copy in loads[:5]:
        copy.start()
    line = [device(x, y, zhi * 4 + (zlo + k) % 4, c) for k in (1, 2, 3)]
    partners = [
        device(x + 1, y, z, c), device(x - 1, y, z, c), device(x + 2, y, z, c),
        device(x, y + 1, z, c), device(x, y - 1, z, c), device(x, y + 2, z, c),
        device(x, y, z + 1, c), device(x, y, z - 1, c), device(x, y, z + 4, c),
        device(x, y, z, c + 1), device(x, y, z + 4, c + 1), *line,
    ]
    barrier = pltpu.get_barrier_semaphore()
    for d in partners:
        pl.semaphore_signal(barrier, inc=1, device_id=d, device_id_type=MESH)

    def remote(src, dst, send, recv, d):
        return pltpu.make_async_remote_copy(src, dst, send, recv, device_id=d, device_id_type=MESH)

    right, left, core = device(x + 1, y, z, c), device(x - 1, y, z, c), device(x, y, z, c + 1)
    xr, xl, xo = (x + 1) % NX, (x - 1) % NX, (x + 2) % NX
    swap = remote(st_hbm, raw.at[rows_of], fsend.at[3], frecv.at[3], core)

    def reduce_plan(n, buf, got):
        def one(k, src, d):
            return remote(src, got.at[k], rsend.at[n, k], rrecv.at[n, k], d)

        return {
            "R1": one(0, buf.at[xo, 0], right), "L1": one(1, buf.at[xo, 1], left),
            "R1b": one(2, buf.at[xr, 1], right), "L1b": one(3, buf.at[xl, 0], left),
            "R2": one(4, buf.at[xr, 0], right), "L2": one(5, buf.at[xl, 1], left),
        }

    def over(n, k, buf, got, rows):
        src, dst = buf.at[x, 1 - zhi, rows], got.at[6, rows]
        return remote(src, dst, rsend.at[n, k], rrecv.at[n, k], device(x, y, z + 4, c))

    first, second = reduce_plan(0, pg, rg), reduce_plan(1, pin, rin)
    early, later = slice(C0, TOK), slice(0, C0)
    first["Zc"] = over(0, 6, pg, rg, early)
    first["Z"] = over(0, 7, pg, rg, later)
    second["Z"] = over(1, 6, pin, rin, slice(0, 32))

    loads[0].wait()
    loads[1].wait()
    pg[...] = jnp.dot(og[...], po[...], preferred_element_type=F32).reshape(pg.shape)
    pl.semaphore_wait(barrier, len(partners))
    for k in ("R1", "L1", "R1b", "L1b"):
        first[k].start()
    loads[2].wait()
    loads[3].wait()
    pin[...] = lax.dot_general(
        pi[...], li[...], (((0,), (1,)), ((), ())), preferred_element_type=F32
    ).reshape(pin.shape)

    position = lax.broadcasted_iota(jnp.int32, (8, 128), 0) * 128 + lax.broadcasted_iota(jnp.int32, (8, 128), 1)
    slots, begin = jnp.zeros((8, 128), F32), jnp.int32(0)
    for k in range(QB):
        end = begin + len_ref[0, k]
        here = (position >= begin) & (position < end)
        slots = slots + jnp.where(here, ord_ref[0, k], 0).astype(F32)
        begin = end
    ins[y, zlo, 128:136, :] = slots

    def halfway(cps, buf, got):
        cps["R1"].wait_recv()
        buf[xr, 0] = buf[xr, 0] + got[0]
        cps["R2"].start()
        cps["L1"].wait_recv()
        buf[xl, 1] = buf[xl, 1] + got[1]
        cps["L2"].start()

    def reduced(cps, buf, got):
        for k in ("R1b", "L1b", "R2", "L2"):
            cps[k].wait_recv()
        for half in (1 - zhi, zhi):
            buf[x, half] = buf[x, half] + (got[3 - half] + got[4 + half])
            if half is not zhi:
                for k in ("Zc", "Z"):
                    if k in cps:
                        cps[k].start()

    halfway(first, pg, rg)
    for k in ("R1", "L1", "R1b", "L1b"):
        second[k].start()
    loads[5].start()
    swap.start()
    reduced(first, pg, rg)
    halfway(second, pin, rin)
    reduced(second, pin, rin)

    plan, needs = gather_plan(me, grads, ins)
    copies = {
        m.name: remote(m.ref, m.ref, gsend.at[n], grecv.at[n], target(me, m)) for n, m in enumerate(plan)
    }

    def prepare(part):
        if part == 0:
            loads[4].wait()
            loads[5].wait()
            swap.wait()

        @pl.loop(part * 4, part * 4 + 4)
        def _(k):
            cols = pl.ds(pl.multiple_of(k * 512, 512), 512)
            high, low = split(raw[:, cols] * inv[:, cols])
            st_hi[:, cols] = high
            st_lo[:, cols] = low

    def outer(r, part):
        by = (y + r) % NY
        high_at = NEAR.index(r) * 64 if r != FAR else 384
        low_at = high_at + (192 if r != FAR else 64)

        @pl.loop(part * 2, part * 2 + 2)
        def _(bz):
            g = split(grads[by, bz].reshape(512, 256))
            mine = ins[by, bz]
            rows = jnp.concatenate([mine[32 * k:32 * k + 32] for k in range(4)], axis=1)
            slot = jnp.concatenate([mine[128 + k:129 + k] for k in range(4)], axis=1)
            member = (slot == lax.broadcasted_iota(jnp.int32, (QB, 512), 0).astype(F32)).astype(F32)
            high = rows.astype(BF16).astype(F32)
            masked = [
                (v[:, None, :] * member[None]).reshape(512, 512).astype(BF16) for v in (high, rows - high)
            ]
            high, low = split(dot3(masked, g, (((1,), (0,)), ((), ()))))
            for i in range(32):
                cols = slice(i * 256, (i + 1) * 256)
                q[pl.ds(pl.multiple_of(high_at + bz * QB, QB), QB), cols] = high[i * QB:(i + 1) * QB]
                q[pl.ds(pl.multiple_of(low_at + bz * QB, QB), QB), cols] = low[i * QB:(i + 1) * QB]

    last = (((1,), (1,)), ((), ()))

    def near_scores(part):
        if part == 0:
            sc[...] = jnp.zeros_like(sc)

        @pl.loop(part * 2, part * 2 + 2)
        def _(k):
            cols = pl.ds(pl.multiple_of(k * 1024, 1024), 1024)
            both = lax.dot_general(q[0:384, cols], st_hi[:, cols], last, preferred_element_type=F32)
            high = lax.dot_general(q[0:192, cols], st_lo[:, cols], last, preferred_element_type=F32)
            total = both[0:192] + both[192:384] + high
            for n, r in enumerate(NEAR):
                to = (y + r) % NX
                sc[to] = sc[to] + total[n * 64:(n + 1) * 64].reshape(2, 32, 384)

    def far_scores():
        def step(k, total):
            cols = pl.ds(pl.multiple_of(k * 1024, 1024), 1024)
            both = lax.dot_general(st_hi[:, cols], q[384:512, cols], last, preferred_element_type=F32)
            high = lax.dot_general(st_lo[:, cols], q[384:448, cols], last, preferred_element_type=F32)
            return total[0] + both, total[1] + high

        both, high = lax.fori_loop(0, 8, step, (jnp.zeros((384, 128), F32), jnp.zeros((384, 64), F32)))
        rows = (both[:, 0:64] + both[:, 64:128] + high).T
        sc[(y + FAR) % NX] = rows.reshape(2, 32, 384)

    def pass_on(r):
        to = (y + r) % NX
        slot = (x - to + NX - 1) % NX

        @pl.when(to != x)
        def _():
            remote(sc.at[to], rsc.at[slot], ssend.at[slot], srecv.at[slot], device(to, y, z, c)).start()

    tasks = [(f"prepare{n}", (), 0.6) for n in range(4)]
    run = {f"prepare{n}": (prepare, (n,)) for n in range(4)}
    done = [f"prepare{n}" for n in range(4)]
    for r in NEAR:
        for n in range(2):
            tasks.append((f"outer{r},{n}", tuple(needs[r]), 1.3))
            run[f"outer{r},{n}"] = (outer, (r, n))
            done.append(f"outer{r},{n}")
    for n in range(4):
        tasks.append((f"near{n}", tuple(done), 1.5))
        run[f"near{n}"] = (near_scores, (n,))
        done.append(f"near{n}")
    for r in NEAR:
        tasks.append((f"pass{r}", tuple(done), 0.1))
        run[f"pass{r}"] = (pass_on, (r,))
    for n in range(2):
        tasks.append((f"outer{FAR},{n}", tuple(done) + tuple(needs[FAR]), 1.3))
        run[f"outer{FAR},{n}"] = (outer, (FAR, n))

    for verb, name in order_of(plan, tasks)[0]:
        if name == "gc":
            first["Zc"].wait_recv()
            grads[y, zlo, x, zhi, early] = pg[x, zhi, early] + rg[6, early]
        elif name == "g":
            first["Z"].wait_recv()
            grads[y, zlo, x, zhi, later] = pg[x, zhi, later] + rg[6, later]
        elif name == "i":
            second["Z"].wait_recv()
            whole = pin[x, zhi] + rin[6]
            for k in range(4):
                ins[y, zlo, 32 * k:32 * k + 32, :] = whole[:, 128 * k:128 * k + 128]
        elif verb == "send":
            copies[name].start()
        elif verb == "wait":
            copies[name].wait_recv()
        else:
            work, given = run[name]
            work(*given)
    far_scores()
    pass_on(FAR)
    for copy in (*first.values(), *second.values(), *copies.values()):
        copy.wait_send()

    sends = [
        remote(sc.at[x], rsc.at[n], ssend.at[n], srecv.at[n], right) for n in range(3)
    ]
    for copy in sends:
        copy.wait_recv()
    sc[x] = sc[x] + (rsc[0] + rsc[1]) + rsc[2]
    ours, others = (pl.ds(pl.multiple_of(k * 128, 128), 256) for k in (c, 1 - c))
    ends = [
        remote(sc.at[x, 1 - zhi, :, ours], fin.at[0], fsend.at[0], frecv.at[0], device(x, y, z + 4, c)),
        remote(sc.at[x, 1 - zhi, :, others], fin.at[1], fsend.at[1], frecv.at[1], device(x, y, z + 4, c + 1)),
        remote(sc.at[x, zhi, :, others], fin.at[2], fsend.at[2], frecv.at[2], core),
    ]
    for copy in ends:
        copy.start()
    for copy in ends:
        copy.wait_recv()
    mine, theirs = (
        jnp.where(c == 0, v[:, 0:192], v[:, 64:256])
        for v in (sc[x, zhi, :, ours] + fin[0], fin[1] + fin[2])
    )
    for half in range(2):
        part = slice(half * QB, (half + 1) * QB)
        out_ref[pl.ds(pl.multiple_of(half * 32 + c * QB, QB), QB), :] = mine[part]
        out_ref[pl.ds(pl.multiple_of(half * 32 + (1 - c) * QB, QB), QB), :] = theirs[part]

    for copy in (*sends, *ends):
        copy.wait_send()


def body(layer_input, out_grad, proj_in, proj_out, inv_diag, stored, seq_lengths, query_order):
    hbm, smem = pl.BlockSpec(memory_space=pl.ANY), pl.BlockSpec(memory_space=pltpu.SMEM)
    dma = pltpu.SemaphoreType.DMA
    return pl.pallas_call(
        kernel,
        out_shape=jax.ShapeDtypeStruct((64, 192), F32),
        in_specs=[hbm] * 6 + [smem] * 2,
        out_specs=pl.BlockSpec(memory_space=pltpu.VMEM),
        scratch_shapes=[
            pltpu.VMEM((512, 1024), BF16),
            pltpu.VMEM((512, 1024), BF16),
            pltpu.VMEM((1024, 256), BF16),
            pltpu.VMEM((1024, 256), BF16),
            pltpu.VMEM((1, 8192), F32),
            pltpu.VMEM((384, 8192), F32),
            pltpu.VMEM((384, 8192), BF16),
            pltpu.VMEM((384, 8192), BF16),
            pltpu.VMEM((4, 2, 64, 256), F32),
            pltpu.VMEM((4, 2, 32, 512), F32),
            pltpu.VMEM((7, 64, 256), F32),
            pltpu.VMEM((7, 32, 512), F32),
            pltpu.VMEM((4, 4, 4, 2, TOK, 256), F32),
            pltpu.VMEM((4, 4, INROWS, 128), F32),
            pltpu.VMEM((512, 8192), BF16),
            pltpu.VMEM((4, 2, 32, 384), F32),
            pltpu.VMEM((3, 2, 32, 384), F32),
            pltpu.VMEM((3, 32, 256), F32),
            dma((6,)),
            dma((176,)), dma((176,)),
            dma((2, 8)), dma((2, 8)),
            dma((3,)), dma((3,)),
            dma((4,)), dma((4,)),
        ],
        compiler_params=pltpu.CompilerParams(
            collective_id=0, has_side_effects=True, vmem_limit_bytes=60 * 2**20
        ),
    )(layer_input, out_grad, proj_in, proj_out, inv_diag.reshape(1, -1), stored, seq_lengths, query_order)


def solution(mesh):
    return jax.shard_map(
        body,
        mesh=mesh,
        in_specs=(
            P("store", "feat"),
            P("store", "feat"),
            P("feat", None),
            P("feat", None),
            P("feat"),
            P("store", "feat"),
            P("store", None),
            P("store", None),
        ),
        out_specs=P("feat", "store"),
        check_vma=False,
    )
```

```python
import heapq

import jax
import jax.numpy as jnp
from jax import lax
from jax.experimental import pallas as pl
from jax.experimental.pallas import tpu as pltpu
from jax.sharding import PartitionSpec as P

MESH = pl.DeviceIdType.MESH
F32, BF16 = jnp.float32, jnp.bfloat16
NX, NY, NZ = 4, 4, 8
QB = 16
A0, B0, C0, TOK = 0, 16, 40, 64
INROWS = 136


def place():
    f, s = lax.axis_index("feat"), lax.axis_index("store")
    return f // 2, s // 8, (f % 2) * 4 + (s // 2) % 4, s % 2


def device(x, y, z, c):
    x, y, z, c = x % NX, y % NY, z % NZ, c % 2
    return (x * 2 + z // 4, y * 8 + (z % 4) * 2 + c)


class Message:
    def __init__(self, name, deps, kb, axis, hop, ref):
        self.name, self.deps, self.kb, self.axis, self.hop, self.ref = name, tuple(deps), kb, axis, hop, ref


def ring(k, sign, tag):
    return f"{tag}{sign * k}"


def around(tag):
    return [ring(k, s, tag) for k in (1, 2, 3, 4) for s in (1, -1)]


NEAR, FAR = (0, 1, -1), 2


def gather_plan(me, grads, ins):
    x, y, z, c = me
    out = []

    def zz(v):
        return v % 4, (v % NZ) // 4

    def add(name, deps, kb, axis, hop, ref):
        out.append(Message(name, deps, kb, axis, hop, ref))

    def ga(zv, yv, xs=slice(None)):
        lo, hi = zz(zv)
        return grads.at[yv % NY, lo, xs, hi, A0:B0, :]

    def gb(zv, yv, xv):
        lo, hi = zz(zv)
        return grads.at[yv % NY, lo, xv % NX, hi, B0:C0, :]

    def gz(xv, yv, rows, zs=slice(None)):
        return grads.at[yv % NY, zs, xv % NX, :, rows, :]

    first, second = pl.ds(0, 2), pl.ds(2, 2)
    brows, crows = slice(B0, C0), slice(C0, TOK)
    ka, kb, kc = (B0 - A0), (C0 - B0), (TOK - C0)
    lo, hi = zz(z)
    from_y = {1: -1, -1: 1, 2: 2}
    for k in (1, 2, 3, 4):
        for sign in (1, -1):
            zlo, zhi = zz(z - sign * (k - 1))
            cols = slice(None) if k < 4 else pl.ds(0 if sign > 0 else 128, 128)
            deps = ["gc"] if k == 1 else [ring(k - 1, sign, "Cz")]
            add(ring(k, sign, "Cz"), deps, kc if k < 4 else kc / 2, "z", sign, grads.at[y, zlo, x, zhi, crows, cols])
    call = ["gc"] + around("Cz")
    for hop in (1, -1, 2):
        add(f"Ax{hop}", ["g"], ka, "x", hop, grads.at[y, lo, x, hi, A0:B0, :])
    aall = ["g"] + [f"Ax{h}" for h in (1, -1, 2)]
    for hop in (1, -1, 2):
        add(f"By{hop}", ["g"], kb, "y", hop, gb(z, y, x))
    for hop in (1, -1, 2):
        add(f"Ay{hop}", aall, 4 * ka, "y", hop, ga(z, y))
    crossed = {s: [f"Cx{s},{d}" for d in (0, -1, 1, -2, 2, -3, 3, 4)] for s in (1, -1)}
    for d in (0, -1, 1, -2, 2, -3, 3, 4):
        deps = ["gc"] if d == 0 else (["Cz4", "Cz-4"] if d == 4 else [f"Cz{-d}"])
        zlo, zhi = zz(z + d)
        for sign in (1, -1):
            add(f"Cx{sign},{d}", deps, kc, "x", sign, grads.at[y, zlo, x, zhi, crows, :])
    for sign in (1, -1):
        half = first if sign > 0 else second
        add(f"Cx{2 * sign}", crossed[sign], 4 * kc, "x", sign, gz(x - sign, y, crows, half))
    for k in (1, 2, 3):
        add(f"Iz{k}", ["i", "Cz3", "Cz-3"], 68, "i", k, ins.at[y, lo])
    iall = ["i"] + [f"Iz{k}" for k in (1, 2, 3)]
    needs = {}
    across = {s: [f"C0y{s},{d}" for d in (0, -1, 1, -2, 2, -3, 3, 4)] for s in (1, -1)}
    for r in (*NEAR, FAR):
        tag = f"B{r}z"
        here = ["g"] if r == 0 else [f"By{from_y[r]}"]
        held = ["B0z3", "B0z-3"] if r == FAR else []
        for k in (1, 2, 3, 4):
            for sign in (1, -1):
                deps = here + held if k == 1 else [ring(k - 1, sign, tag)]
                zv = z - sign * (k - 1)
                ref = gb(zv, y + r, x)
                if k == 4:
                    zlo, zhi = zz(zv)
                    ref = grads.at[(y + r) % NY, zlo, x, zhi, brows, pl.ds(0 if sign > 0 else 128, 128)]
                add(ring(k, sign, tag), deps, kb if k < 4 else kb / 2, "z", sign, ref)
        ball = here + around(tag)
        brought = []
        if r == 0:
            for d in (0, -1, 1, -2, 2, -3, 3, 4):
                deps = ["g"] if d == 0 else ([ring(4, 1, tag), ring(4, -1, tag)] if d == 4 else [f"{tag}{-d}"])
                for sign in (1, -1):
                    add(f"B0x{sign},{d}", deps, kb, "x", sign, gb(z + d, y, x))
            came = {s: [f"B0x{s},{d}" for d in (0, -1, 1, -2, 2, -3, 3, 4)] for s in (1, -1)}
        else:
            for sign in (1, -1):
                add(f"B{r}x{sign}", ball + (["B1x1", "B1x-1"] if r == FAR else []), 8 * kb, "x", sign, gz(x, y + r, brows))
            came = {s: [f"B{r}x{s}"] for s in (1, -1)}
        for sign in (1, -1):
            half = first if sign > 0 else second
            add(f"B{r}x{2 * sign}", came[sign], 4 * kb, "x", sign, gz(x - sign, y + r, brows, half))
            brought += came[sign] + [f"B{r}x{2 * sign}"]
        tag = f"A{r}z"
        here = aall if r == 0 else [f"Ay{from_y[r]}"]
        held = ["A0z3", "A0z-3"] if r == FAR else ["B1z3", "B1z-3"]
        for k in (1, 2, 3, 4):
            for sign in (1, -1):
                deps = here + held if k == 1 else [ring(k - 1, sign, tag)]
                xs = slice(None) if k < 4 else (first if sign > 0 else second)
                ref = ga(z - sign * (k - 1), y + r, xs)
                add(ring(k, sign, tag), deps, 4 * ka if k < 4 else 2 * ka, "z", sign, ref)
        needs[r] = ball + brought + here + around(tag)
        if r == 0:
            needs[r] += call + crossed[1] + crossed[-1] + ["Cx2", "Cx-2"] + iall
            for d in (0, -1, 1, -2, 2, -3, 3, 4):
                deps = ["gc"] if d == 0 else (["Cz4", "Cz-4"] if d == 4 else [f"Cz{-d}"])
                zlo, zhi = zz(z + d)
                for sign in (1, -1):
                    add(f"C0y{sign},{d}", deps, kc, "y", sign, grads.at[y, zlo, x, zhi, crows, :])
            for d in (-1, 1, 2):
                deps = ["Cx2", "Cx-2"] if d == 2 else crossed[-d]
                for sign in (1, -1):
                    add(f"C{d}y{sign}", deps, 8 * kc, "y", sign, gz(x + d, y, crows))
            for sign in (1, -1):
                add(f"Iy{sign}", iall, 272, "y", sign, ins.at[y])
        elif r != FAR:
            sign = from_y[r]
            needs[r] += [f"C{d}y{sign}" for d in (-1, 1, 2)] + across[sign] + [f"Iy{sign}"]
        else:
            for sign in (1, -1):
                half = first if sign > 0 else second
                add(f"Iy{2 * sign}", [f"Iy{sign}", f"C2y{sign}"], 136, "y", sign, ins.at[(y - sign) % NY, half])
                needs[r] += [f"Iy{2 * sign}"]
            for sign in (1, -1):
                half = first if sign > 0 else second
                add(f"C2x{sign}", [f"C{-sign}y{2 * sign}"], 4 * kc, "x", sign, gz(x - sign, y + FAR, crows, half))
                needs[r] += [f"C2x{sign}"]
            for d in (-1, 1, 0):
                for sign in (1, -1):
                    half = first if sign > 0 else second
                    deps = (across[sign] if d == 0 else [f"C{d}y{sign}"]) + [f"C1y{sign}"]
                    add(f"C{d}y{2 * sign}", deps, 4 * kc, "y", sign, gz(x + d, y - sign, crows, half))
                    needs[r] += [f"C{d}y{2 * sign}"]
    return out, needs


def target(me, m):
    x, y, z, c = me
    if m.axis == "x":
        return device(x + m.hop, y, z, c)
    if m.axis == "y":
        return device(x, y + m.hop, z, c)
    if m.axis == "z":
        return device(x, y, z + m.hop, c)
    return device(x, y, (z // 4) * 4 + (z % 4 + m.hop) % 4, c)


def order_of(plan, tasks, rate=32.0, latency=2.0, late=5.0):
    free, got, sent, events, steps = {}, set(), set(), [(0.0, 0, "gc"), (1.2, 1, "g"), (late, 2, "i")], []
    heapq.heapify(events)
    count, now, todo = 3, 0.0, list(tasks)
    while events or todo:
        ready = next((t for t in todo if all(d in got for d in t[1])), None)
        if ready and not (events and events[0][0] <= now):
            todo.remove(ready)
            steps.append(("task", ready[0]))
            got.add(ready[0])
            now += ready[2]
            continue
        at, _, name = heapq.heappop(events)
        now = max(now, at)
        got.add(name)
        steps.append(("wait", name))
        for m in plan:
            if m.name in sent or not all(d in got for d in m.deps):
                continue
            sent.add(m.name)
            steps.append(("send", m.name))
            if m.axis == "i":
                links, kb = ("z+", "z-"), m.kb
            elif abs(m.hop) > 1:
                links, kb = (m.axis + "+", m.axis + "-"), m.kb
            else:
                links, kb = ((m.axis + "+",) if m.hop > 0 else (m.axis + "-",)), m.kb
            end = max(now, *(free.get(k, 0.0) for k in links)) + kb / rate
            for k in links:
                free[k] = end
            heapq.heappush(events, (end + latency, count, m.name))
            count += 1
    return steps, now


def split(v):
    high = v.astype(BF16)
    return high, (v - high.astype(F32)).astype(BF16)


def dot3(a, b, dims):
    (ah, al), (bh, bl) = a, b
    return (
        lax.dot_general(ah, bh, dims, preferred_element_type=F32)
        + lax.dot_general(ah, bl, dims, preferred_element_type=F32)
        + lax.dot_general(al, bh, dims, preferred_element_type=F32)
    )


def kernel(
    li_hbm, og_hbm, pi_hbm, po_hbm, inv_hbm, st_hbm, len_ref, ord_ref, out_ref,
    li, og, pi, po, inv, raw, st_hi, st_lo, pg, pin, rg, rin, grads, ins, q, sc, rsc, fin,
    load_sem, gsend, grecv, rsend, rrecv, ssend, srecv, fsend, frecv,
):
    me = x, y, z, c = place()
    zlo, zhi = z % 4, z // 4
    rows_of = pl.ds(pl.multiple_of(c * 192, 192), 192)
    loads = [
        pltpu.make_async_copy(src, dst, load_sem.at[n])
        for n, (src, dst) in enumerate(
            ((og_hbm, og), (po_hbm, po), (li_hbm, li), (pi_hbm, pi), (inv_hbm, inv), (st_hbm, raw.at[rows_of]))
        )
    ]
    for copy in loads[:5]:
        copy.start()
    line = [device(x, y, zhi * 4 + (zlo + k) % 4, c) for k in (1, 2, 3)]
    partners = [
        device(x + 1, y, z, c), device(x - 1, y, z, c), device(x + 2, y, z, c),
        device(x, y + 1, z, c), device(x, y - 1, z, c), device(x, y + 2, z, c),
        device(x, y, z + 1, c), device(x, y, z - 1, c), device(x, y, z + 4, c),
        device(x, y, z, c + 1), device(x, y, z + 4, c + 1), *line,
    ]
    barrier = pltpu.get_barrier_semaphore()
    for d in partners:
        pl.semaphore_signal(barrier, inc=1, device_id=d, device_id_type=MESH)

    def remote(src, dst, send, recv, d):
        return pltpu.make_async_remote_copy(src, dst, send, recv, device_id=d, device_id_type=MESH)

    right, left, core = device(x + 1, y, z, c), device(x - 1, y, z, c), device(x, y, z, c + 1)
    xr, xl, xo = (x + 1) % NX, (x - 1) % NX, (x + 2) % NX
    swap = remote(st_hbm, raw.at[rows_of], fsend.at[3], frecv.at[3], core)

    def reduce_plan(n, buf, got):
        def one(k, src, d):
            return remote(src, got.at[k], rsend.at[n, k], rrecv.at[n, k], d)

        return {
            "R1": one(0, buf.at[xo, 0], right), "L1": one(1, buf.at[xo, 1], left),
            "R1b": one(2, buf.at[xr, 1], right), "L1b": one(3, buf.at[xl, 0], left),
            "R2": one(4, buf.at[xr, 0], right), "L2": one(5, buf.at[xl, 1], left),
        }

    def over(n, k, buf, got, rows):
        src, dst = buf.at[x, 1 - zhi, rows], got.at[6, rows]
        return remote(src, dst, rsend.at[n, k], rrecv.at[n, k], device(x, y, z + 4, c))

    first, second = reduce_plan(0, pg, rg), reduce_plan(1, pin, rin)
    early, later = slice(C0, TOK), slice(0, C0)
    first["Zc"] = over(0, 6, pg, rg, early)
    first["Z"] = over(0, 7, pg, rg, later)
    second["Z"] = over(1, 6, pin, rin, slice(0, 32))

    loads[0].wait()
    loads[1].wait()
    pg[...] = jnp.dot(og[...], po[...], preferred_element_type=F32).reshape(pg.shape)
    pl.semaphore_wait(barrier, len(partners))
    for k in ("R1", "L1", "R1b", "L1b"):
        first[k].start()
    loads[2].wait()
    loads[3].wait()
    pin[...] = lax.dot_general(
        pi[...], li[...], (((0,), (1,)), ((), ())), preferred_element_type=F32
    ).reshape(pin.shape)

    position = lax.broadcasted_iota(jnp.int32, (8, 128), 0) * 128 + lax.broadcasted_iota(jnp.int32, (8, 128), 1)
    slots, begin = jnp.zeros((8, 128), F32), jnp.int32(0)
    for k in range(QB):
        end = begin + len_ref[0, k]
        here = (position >= begin) & (position < end)
        slots = slots + jnp.where(here, ord_ref[0, k], 0).astype(F32)
        begin = end
    ins[y, zlo, 128:136, :] = slots

    def halfway(cps, buf, got):
        cps["R1"].wait_recv()
        buf[xr, 0] = buf[xr, 0] + got[0]
        cps["R2"].start()
        cps["L1"].wait_recv()
        buf[xl, 1] = buf[xl, 1] + got[1]
        cps["L2"].start()

    def reduced(cps, buf, got):
        for k in ("R1b", "L1b", "R2", "L2"):
            cps[k].wait_recv()
        for half in (1 - zhi, zhi):
            buf[x, half] = buf[x, half] + (got[3 - half] + got[4 + half])
            if half is not zhi:
                for k in ("Zc", "Z"):
                    if k in cps:
                        cps[k].start()

    halfway(first, pg, rg)
    for k in ("R1", "L1", "R1b", "L1b"):
        second[k].start()
    loads[5].start()
    swap.start()
    reduced(first, pg, rg)
    halfway(second, pin, rin)
    reduced(second, pin, rin)

    plan, needs = gather_plan(me, grads, ins)
    copies = {
        m.name: remote(m.ref, m.ref, gsend.at[n], grecv.at[n], target(me, m)) for n, m in enumerate(plan)
    }

    def prepare(part):
        if part == 0:
            loads[4].wait()
            loads[5].wait()
            swap.wait()

        @pl.loop(part * 4, part * 4 + 4)
        def _(k):
            cols = pl.ds(pl.multiple_of(k * 512, 512), 512)
            high, low = split(raw[:, cols] * inv[:, cols])
            st_hi[:, cols] = high
            st_lo[:, cols] = low

    def outer(r, part):
        by = (y + r) % NY
        high_at = NEAR.index(r) * 64 if r != FAR else 384
        low_at = high_at + (192 if r != FAR else 64)

        @pl.loop(part * 2, part * 2 + 2)
        def _(bz):
            g = split(grads[by, bz].reshape(512, 256))
            mine = ins[by, bz]
            rows = jnp.concatenate([mine[32 * k:32 * k + 32] for k in range(4)], axis=1)
            slot = jnp.concatenate([mine[128 + k:129 + k] for k in range(4)], axis=1)
            member = (slot == lax.broadcasted_iota(jnp.int32, (QB, 512), 0).astype(F32)).astype(F32)
            high = rows.astype(BF16).astype(F32)
            masked = [
                (v[:, None, :] * member[None]).reshape(512, 512).astype(BF16) for v in (high, rows - high)
            ]
            high, low = split(dot3(masked, g, (((1,), (0,)), ((), ()))))
            for i in range(32):
                cols = slice(i * 256, (i + 1) * 256)
                q[pl.ds(pl.multiple_of(high_at + bz * QB, QB), QB), cols] = high[i * QB:(i + 1) * QB]
                q[pl.ds(pl.multiple_of(low_at + bz * QB, QB), QB), cols] = low[i * QB:(i + 1) * QB]

    last = (((1,), (1,)), ((), ()))

    def near_scores(part):
        if part == 0:
            sc[...] = jnp.zeros_like(sc)

        @pl.loop(part * 2, part * 2 + 2)
        def _(k):
            cols = pl.ds(pl.multiple_of(k * 1024, 1024), 1024)
            both = lax.dot_general(q[0:384, cols], st_hi[:, cols], last, preferred_element_type=F32)
            high = lax.dot_general(q[0:192, cols], st_lo[:, cols], last, preferred_element_type=F32)
            total = both[0:192] + both[192:384] + high
            for n, r in enumerate(NEAR):
                to = (y + r) % NX
                sc[to] = sc[to] + total[n * 64:(n + 1) * 64].reshape(2, 32, 384)

    def far_scores():
        def step(k, total):
            cols = pl.ds(pl.multiple_of(k * 1024, 1024), 1024)
            both = lax.dot_general(st_hi[:, cols], q[384:512, cols], last, preferred_element_type=F32)
            high = lax.dot_general(st_lo[:, cols], q[384:448, cols], last, preferred_element_type=F32)
            return total[0] + both, total[1] + high

        both, high = lax.fori_loop(0, 8, step, (jnp.zeros((384, 128), F32), jnp.zeros((384, 64), F32)))
        rows = (both[:, 0:64] + both[:, 64:128] + high).T
        sc[(y + FAR) % NX] = rows.reshape(2, 32, 384)

    def pass_on(r):
        to = (y + r) % NX
        slot = (x - to + NX - 1) % NX

        @pl.when(to != x)
        def _():
            remote(sc.at[to], rsc.at[slot], ssend.at[slot], srecv.at[slot], device(to, y, z, c)).start()

    tasks = [(f"prepare{n}", (), 0.6) for n in range(4)]
    run = {f"prepare{n}": (prepare, (n,)) for n in range(4)}
    done = [f"prepare{n}" for n in range(4)]
    for r in NEAR:
        for n in range(2):
            tasks.append((f"outer{r},{n}", tuple(needs[r]), 1.3))
            run[f"outer{r},{n}"] = (outer, (r, n))
            done.append(f"outer{r},{n}")
    for n in range(4):
        tasks.append((f"near{n}", tuple(done), 1.5))
        run[f"near{n}"] = (near_scores, (n,))
        done.append(f"near{n}")
    for r in NEAR:
        tasks.append((f"pass{r}", tuple(done) + tuple(needs[FAR]), 0.1))
        run[f"pass{r}"] = (pass_on, (r,))
    for n in range(2):
        tasks.append((f"outer{FAR},{n}", tuple(done) + tuple(needs[FAR]), 1.3))
        run[f"outer{FAR},{n}"] = (outer, (FAR, n))

    for verb, name in order_of(plan, tasks)[0]:
        if name == "gc":
            first["Zc"].wait_recv()
            grads[y, zlo, x, zhi, early] = pg[x, zhi, early] + rg[6, early]
        elif name == "g":
            first["Z"].wait_recv()
            grads[y, zlo, x, zhi, later] = pg[x, zhi, later] + rg[6, later]
        elif name == "i":
            second["Z"].wait_recv()
            whole = pin[x, zhi] + rin[6]
            for k in range(4):
                ins[y, zlo, 32 * k:32 * k + 32, :] = whole[:, 128 * k:128 * k + 128]
        elif verb == "send":
            copies[name].start()
        elif verb == "wait":
            copies[name].wait_recv()
        else:
            work, given = run[name]
            work(*given)
    far_scores()
    pass_on(FAR)
    for copy in (*first.values(), *second.values(), *copies.values()):
        copy.wait_send()

    sends = [
        remote(sc.at[x], rsc.at[n], ssend.at[n], srecv.at[n], right) for n in range(3)
    ]
    for copy in sends:
        copy.wait_recv()
    sc[x] = sc[x] + (rsc[0] + rsc[1]) + rsc[2]
    ours, others = (pl.ds(pl.multiple_of(k * 128, 128), 256) for k in (c, 1 - c))
    ends = [
        remote(sc.at[x, 1 - zhi, :, ours], fin.at[0], fsend.at[0], frecv.at[0], device(x, y, z + 4, c)),
        remote(sc.at[x, 1 - zhi, :, others], fin.at[1], fsend.at[1], frecv.at[1], device(x, y, z + 4, c + 1)),
        remote(sc.at[x, zhi, :, others], fin.at[2], fsend.at[2], frecv.at[2], core),
    ]
    for copy in ends:
        copy.start()
    for copy in ends:
        copy.wait_recv()
    mine, theirs = (
        jnp.where(c == 0, v[:, 0:192], v[:, 64:256])
        for v in (sc[x, zhi, :, ours] + fin[0], fin[1] + fin[2])
    )
    for half in range(2):
        part = slice(half * QB, (half + 1) * QB)
        out_ref[pl.ds(pl.multiple_of(half * 32 + c * QB, QB), QB), :] = mine[part]
        out_ref[pl.ds(pl.multiple_of(half * 32 + (1 - c) * QB, QB), QB), :] = theirs[part]

    for copy in (*sends, *ends):
        copy.wait_send()


def body(layer_input, out_grad, proj_in, proj_out, inv_diag, stored, seq_lengths, query_order):
    hbm, smem = pl.BlockSpec(memory_space=pl.ANY), pl.BlockSpec(memory_space=pltpu.SMEM)
    dma = pltpu.SemaphoreType.DMA
    return pl.pallas_call(
        kernel,
        out_shape=jax.ShapeDtypeStruct((64, 192), F32),
        in_specs=[hbm] * 6 + [smem] * 2,
        out_specs=pl.BlockSpec(memory_space=pltpu.VMEM),
        scratch_shapes=[
            pltpu.VMEM((512, 1024), BF16),
            pltpu.VMEM((512, 1024), BF16),
            pltpu.VMEM((1024, 256), BF16),
            pltpu.VMEM((1024, 256), BF16),
            pltpu.VMEM((1, 8192), F32),
            pltpu.VMEM((384, 8192), F32),
            pltpu.VMEM((384, 8192), BF16),
            pltpu.VMEM((384, 8192), BF16),
            pltpu.VMEM((4, 2, 64, 256), F32),
            pltpu.VMEM((4, 2, 32, 512), F32),
            pltpu.VMEM((7, 64, 256), F32),
            pltpu.VMEM((7, 32, 512), F32),
            pltpu.VMEM((4, 4, 4, 2, TOK, 256), F32),
            pltpu.VMEM((4, 4, INROWS, 128), F32),
            pltpu.VMEM((512, 8192), BF16),
            pltpu.VMEM((4, 2, 32, 384), F32),
            pltpu.VMEM((3, 2, 32, 384), F32),
            pltpu.VMEM((3, 32, 256), F32),
            dma((6,)),
            dma((176,)), dma((176,)),
            dma((2, 8)), dma((2, 8)),
            dma((3,)), dma((3,)),
            dma((4,)), dma((4,)),
        ],
        compiler_params=pltpu.CompilerParams(
            collective_id=0, has_side_effects=True, vmem_limit_bytes=60 * 2**20
        ),
    )(layer_input, out_grad, proj_in, proj_out, inv_diag.reshape(1, -1), stored, seq_lengths, query_order)


def solution(mesh):
    return jax.shard_map(
        body,
        mesh=mesh,
        in_specs=(
            P("store", "feat"),
            P("store", "feat"),
            P("feat", None),
            P("feat", None),
            P("feat"),
            P("store", "feat"),
            P("store", None),
            P("store", None),
        ),
        out_specs=P("feat", "store"),
        check_vma=False,
    )
```

```python
import heapq

import jax
import jax.numpy as jnp
from jax import lax
from jax.experimental import pallas as pl
from jax.experimental.pallas import tpu as pltpu
from jax.sharding import PartitionSpec as P

MESH = pl.DeviceIdType.MESH
F32, BF16 = jnp.float32, jnp.bfloat16
NX, NY, NZ = 4, 4, 8
QB = 16
A0, B0, C0, TOK = 0, 16, 40, 64
INROWS = 136


def place():
    f, s = lax.axis_index("feat"), lax.axis_index("store")
    return f // 2, s // 8, (f % 2) * 4 + (s // 2) % 4, s % 2


def device(x, y, z, c):
    x, y, z, c = x % NX, y % NY, z % NZ, c % 2
    return (x * 2 + z // 4, y * 8 + (z % 4) * 2 + c)


class Message:
    def __init__(self, name, deps, kb, axis, hop, ref):
        self.name, self.deps, self.kb, self.axis, self.hop, self.ref = name, tuple(deps), kb, axis, hop, ref


def ring(k, sign, tag):
    return f"{tag}{sign * k}"


def around(tag):
    return [ring(k, s, tag) for k in (1, 2, 3, 4) for s in (1, -1)]


NEAR, FAR = (0, 1, -1), 2


def gather_plan(me, grads, ins):
    x, y, z, c = me
    out = []

    def zz(v):
        return v % 4, (v % NZ) // 4

    def add(name, deps, kb, axis, hop, ref):
        out.append(Message(name, deps, kb, axis, hop, ref))

    def ga(zv, yv, xs=slice(None)):
        lo, hi = zz(zv)
        return grads.at[yv % NY, lo, xs, hi, A0:B0, :]

    def gb(zv, yv, xv):
        lo, hi = zz(zv)
        return grads.at[yv % NY, lo, xv % NX, hi, B0:C0, :]

    def gz(xv, yv, rows, zs=slice(None)):
        return grads.at[yv % NY, zs, xv % NX, :, rows, :]

    first, second = pl.ds(0, 2), pl.ds(2, 2)
    brows, crows = slice(B0, C0), slice(C0, TOK)
    ka, kb, kc = (B0 - A0), (C0 - B0), (TOK - C0)
    lo, hi = zz(z)
    from_y = {1: -1, -1: 1, 2: 2}
    for k in (1, 2, 3, 4):
        for sign in (1, -1):
            zlo, zhi = zz(z - sign * (k - 1))
            cols = slice(None) if k < 4 else pl.ds(0 if sign > 0 else 128, 128)
            deps = ["gc"] if k == 1 else [ring(k - 1, sign, "Cz")]
            add(ring(k, sign, "Cz"), deps, kc if k < 4 else kc / 2, "z", sign, grads.at[y, zlo, x, zhi, crows, cols])
    call = ["gc"] + around("Cz")
    for hop in (1, -1, 2):
        add(f"Ax{hop}", ["g"], ka, "x", hop, grads.at[y, lo, x, hi, A0:B0, :])
    aall = ["g"] + [f"Ax{h}" for h in (1, -1, 2)]
    for hop in (1, -1, 2):
        add(f"By{hop}", ["g"], kb, "y", hop, gb(z, y, x))
    for hop in (1, -1, 2):
        add(f"Ay{hop}", aall, 4 * ka, "y", hop, ga(z, y))
    crossed = {s: [f"Cx{s},{d}" for d in (0, -1, 1, -2, 2, -3, 3, 4)] for s in (1, -1)}
    for d in (0, -1, 1, -2, 2, -3, 3, 4):
        deps = ["gc"] if d == 0 else (["Cz4", "Cz-4"] if d == 4 else [f"Cz{-d}"])
        zlo, zhi = zz(z + d)
        for sign in (1, -1):
            add(f"Cx{sign},{d}", deps, kc, "x", sign, grads.at[y, zlo, x, zhi, crows, :])
    for sign in (1, -1):
        half = first if sign > 0 else second
        add(f"Cx{2 * sign}", crossed[sign], 4 * kc, "x", sign, gz(x - sign, y, crows, half))
    for k in (1, 2, 3):
        add(f"Iz{k}", ["i", "Cz3", "Cz-3"], 68, "i", k, ins.at[y, lo])
    iall = ["i"] + [f"Iz{k}" for k in (1, 2, 3)]
    needs = {}
    across = {s: [f"C0y{s},{d}" for d in (0, -1, 1, -2, 2, -3, 3, 4)] for s in (1, -1)}
    for r in (*NEAR, FAR):
        tag = f"B{r}z"
        here = ["g"] if r == 0 else [f"By{from_y[r]}"]
        held = ["B0z3", "B0z-3"] if r == FAR else []
        for k in (1, 2, 3, 4):
            for sign in (1, -1):
                deps = here + held if k == 1 else [ring(k - 1, sign, tag)]
                zv = z - sign * (k - 1)
                ref = gb(zv, y + r, x)
                if k == 4:
                    zlo, zhi = zz(zv)
                    ref = grads.at[(y + r) % NY, zlo, x, zhi, brows, pl.ds(0 if sign > 0 else 128, 128)]
                add(ring(k, sign, tag), deps, kb if k < 4 else kb / 2, "z", sign, ref)
        ball = here + around(tag)
        brought = []
        if r == 0:
            for d in (0, -1, 1, -2, 2, -3, 3, 4):
                deps = ["g"] if d == 0 else ([ring(4, 1, tag), ring(4, -1, tag)] if d == 4 else [f"{tag}{-d}"])
                for sign in (1, -1):
                    add(f"B0x{sign},{d}", deps, kb, "x", sign, gb(z + d, y, x))
            came = {s: [f"B0x{s},{d}" for d in (0, -1, 1, -2, 2, -3, 3, 4)] for s in (1, -1)}
        else:
            for sign in (1, -1):
                add(f"B{r}x{sign}", ball + (["B1x1", "B1x-1"] if r == FAR else []), 8 * kb, "x", sign, gz(x, y + r, brows))
            came = {s: [f"B{r}x{s}"] for s in (1, -1)}
        for sign in (1, -1):
            half = first if sign > 0 else second
            add(f"B{r}x{2 * sign}", came[sign], 4 * kb, "x", sign, gz(x - sign, y + r, brows, half))
            brought += came[sign] + [f"B{r}x{2 * sign}"]
        tag = f"A{r}z"
        here = aall if r == 0 else [f"Ay{from_y[r]}"]
        held = ["A0z3", "A0z-3"] if r == FAR else ["B1z3", "B1z-3"]
        for k in (1, 2, 3, 4):
            for sign in (1, -1):
                deps = here + held if k == 1 else [ring(k - 1, sign, tag)]
                xs = slice(None) if k < 4 else (first if sign > 0 else second)
                ref = ga(z - sign * (k - 1), y + r, xs)
                add(ring(k, sign, tag), deps, 4 * ka if k < 4 else 2 * ka, "z", sign, ref)
        needs[r] = ball + brought + here + around(tag)
        if r == 0:
            needs[r] += call + crossed[1] + crossed[-1] + ["Cx2", "Cx-2"] + iall
            for d in (0, -1, 1, -2, 2, -3, 3, 4):
                deps = ["gc"] if d == 0 else (["Cz4", "Cz-4"] if d == 4 else [f"Cz{-d}"])
                zlo, zhi = zz(z + d)
                for sign in (1, -1):
                    add(f"C0y{sign},{d}", deps, kc, "y", sign, grads.at[y, zlo, x, zhi, crows, :])
            for d in (-1, 1, 2):
                deps = ["Cx2", "Cx-2"] if d == 2 else crossed[-d]
                for sign in (1, -1):
                    add(f"C{d}y{sign}", deps, 8 * kc, "y", sign, gz(x + d, y, crows))
            for sign in (1, -1):
                add(f"Iy{sign}", iall, 272, "y", sign, ins.at[y])
        elif r != FAR:
            sign = from_y[r]
            needs[r] += [f"C{d}y{sign}" for d in (-1, 1, 2)] + across[sign] + [f"Iy{sign}"]
        else:
            for sign in (1, -1):
                half = first if sign > 0 else second
                add(f"Iy{2 * sign}", [f"Iy{sign}", f"C2y{sign}"], 136, "y", sign, ins.at[(y - sign) % NY, half])
                needs[r] += [f"Iy{2 * sign}"]
            for sign in (1, -1):
                half = first if sign > 0 else second
                add(f"C2x{sign}", [f"C{-sign}y{2 * sign}"], 4 * kc, "x", sign, gz(x - sign, y + FAR, crows, half))
                needs[r] += [f"C2x{sign}"]
            for d in (-1, 1, 0):
                for sign in (1, -1):
                    half = first if sign > 0 else second
                    deps = (across[sign] if d == 0 else [f"C{d}y{sign}"]) + [f"C1y{sign}"]
                    add(f"C{d}y{2 * sign}", deps, 4 * kc, "y", sign, gz(x + d, y - sign, crows, half))
                    needs[r] += [f"C{d}y{2 * sign}"]
    return out, needs


def target(me, m):
    x, y, z, c = me
    if m.axis == "x":
        return device(x + m.hop, y, z, c)
    if m.axis == "y":
        return device(x, y + m.hop, z, c)
    if m.axis == "z":
        return device(x, y, z + m.hop, c)
    return device(x, y, (z // 4) * 4 + (z % 4 + m.hop) % 4, c)


def order_of(plan, tasks, rate=32.0, latency=2.0, late=5.0):
    free, got, sent, events, steps = {}, set(), set(), [(0.0, 0, "gc"), (1.2, 1, "g"), (late, 2, "i")], []
    heapq.heapify(events)
    count, now, todo = 3, 0.0, list(tasks)
    while events or todo:
        ready = next((t for t in todo if all(d in got for d in t[1])), None)
        if ready and not (events and events[0][0] <= now):
            todo.remove(ready)
            steps.append(("task", ready[0]))
            got.add(ready[0])
            now += ready[2]
            continue
        at, _, name = heapq.heappop(events)
        now = max(now, at)
        got.add(name)
        steps.append(("wait", name))
        for m in plan:
            if m.name in sent or not all(d in got for d in m.deps):
                continue
            sent.add(m.name)
            steps.append(("send", m.name))
            if m.axis == "i":
                links, kb = ("z+", "z-"), m.kb
            elif abs(m.hop) > 1:
                links, kb = (m.axis + "+", m.axis + "-"), m.kb
            else:
                links, kb = ((m.axis + "+",) if m.hop > 0 else (m.axis + "-",)), m.kb
            end = max(now, *(free.get(k, 0.0) for k in links)) + kb / rate
            for k in links:
                free[k] = end
            heapq.heappush(events, (end + latency, count, m.name))
            count += 1
    return steps, now


def split(v):
    high = v.astype(BF16)
    return high, (v - high.astype(F32)).astype(BF16)


def dot3(a, b, dims):
    (ah, al), (bh, bl) = a, b
    return (
        lax.dot_general(ah, bh, dims, preferred_element_type=F32)
        + lax.dot_general(ah, bl, dims, preferred_element_type=F32)
        + lax.dot_general(al, bh, dims, preferred_element_type=F32)
    )


def kernel(
    li_hbm, og_hbm, pi_hbm, po_hbm, inv_hbm, st_hbm, len_ref, ord_ref, out_ref,
    li, og, pi, po, inv, raw, st_hi, st_lo, pg, pin, rg, rin, grads, ins, q, sc, rsc, fin,
    load_sem, gsend, grecv, rsend, rrecv, ssend, srecv, fsend, frecv,
):
    me = x, y, z, c = place()
    zlo, zhi = z % 4, z // 4
    rows_of = pl.ds(pl.multiple_of(c * 192, 192), 192)
    loads = [
        pltpu.make_async_copy(src, dst, load_sem.at[n])
        for n, (src, dst) in enumerate(
            ((og_hbm, og), (po_hbm, po), (li_hbm, li), (pi_hbm, pi), (inv_hbm, inv), (st_hbm, raw.at[rows_of]))
        )
    ]
    for copy in loads[:5]:
        copy.start()
    line = [device(x, y, zhi * 4 + (zlo + k) % 4, c) for k in (1, 2, 3)]
    partners = [
        device(x + 1, y, z, c), device(x - 1, y, z, c), device(x + 2, y, z, c),
        device(x, y + 1, z, c), device(x, y - 1, z, c), device(x, y + 2, z, c),
        device(x, y, z + 1, c), device(x, y, z - 1, c), device(x, y, z + 4, c),
        device(x, y, z, c + 1), device(x, y, z + 4, c + 1), *line,
    ]
    barrier = pltpu.get_barrier_semaphore()
    for d in partners:
        pl.semaphore_signal(barrier, inc=1, device_id=d, device_id_type=MESH)

    def remote(src, dst, send, recv, d):
        return pltpu.make_async_remote_copy(src, dst, send, recv, device_id=d, device_id_type=MESH)

    right, left, core = device(x + 1, y, z, c), device(x - 1, y, z, c), device(x, y, z, c + 1)
    xr, xl, xo = (x + 1) % NX, (x - 1) % NX, (x + 2) % NX
    swap = remote(st_hbm, raw.at[rows_of], fsend.at[3], frecv.at[3], core)

    def reduce_plan(n, buf, got):
        def one(k, src, d):
            return remote(src, got.at[k], rsend.at[n, k], rrecv.at[n, k], d)

        return {
            "R1": one(0, buf.at[xo, 0], right), "L1": one(1, buf.at[xo, 1], left),
            "R1b": one(2, buf.at[xr, 1], right), "L1b": one(3, buf.at[xl, 0], left),
            "R2": one(4, buf.at[xr, 0], right), "L2": one(5, buf.at[xl, 1], left),
        }

    def over(n, k, buf, got, rows):
        src, dst = buf.at[x, 1 - zhi, rows], got.at[6, rows]
        return remote(src, dst, rsend.at[n, k], rrecv.at[n, k], device(x, y, z + 4, c))

    first, second = reduce_plan(0, pg, rg), reduce_plan(1, pin, rin)
    early, later = slice(C0, TOK), slice(0, C0)
    first["Zc"] = over(0, 6, pg, rg, early)
    first["Z"] = over(0, 7, pg, rg, later)
    second["Z"] = over(1, 6, pin, rin, slice(0, 32))

    loads[0].wait()
    loads[1].wait()
    pg[...] = jnp.dot(og[...], po[...], preferred_element_type=F32).reshape(pg.shape)
    pl.semaphore_wait(barrier, len(partners))
    for k in ("R1", "L1", "R1b", "L1b"):
        first[k].start()
    loads[2].wait()
    loads[3].wait()
    pin[...] = lax.dot_general(
        pi[...], li[...], (((0,), (1,)), ((), ())), preferred_element_type=F32
    ).reshape(pin.shape)

    position = lax.broadcasted_iota(jnp.int32, (8, 128), 0) * 128 + lax.broadcasted_iota(jnp.int32, (8, 128), 1)
    slots, begin = jnp.zeros((8, 128), F32), jnp.int32(0)
    for k in range(QB):
        end = begin + len_ref[0, k]
        here = (position >= begin) & (position < end)
        slots = slots + jnp.where(here, ord_ref[0, k], 0).astype(F32)
        begin = end
    ins[y, zlo, 128:136, :] = slots

    def halfway(cps, buf, got):
        cps["R1"].wait_recv()
        buf[xr, 0] = buf[xr, 0] + got[0]
        cps["R2"].start()
        cps["L1"].wait_recv()
        buf[xl, 1] = buf[xl, 1] + got[1]
        cps["L2"].start()

    def reduced(cps, buf, got):
        for k in ("R1b", "L1b", "R2", "L2"):
            cps[k].wait_recv()
        for half in (1 - zhi, zhi):
            buf[x, half] = buf[x, half] + (got[3 - half] + got[4 + half])
            if half is not zhi:
                for k in ("Zc", "Z"):
                    if k in cps:
                        cps[k].start()

    halfway(first, pg, rg)
    for k in ("R1", "L1", "R1b", "L1b"):
        second[k].start()
    loads[5].start()
    swap.start()
    reduced(first, pg, rg)
    halfway(second, pin, rin)
    reduced(second, pin, rin)

    plan, needs = gather_plan(me, grads, ins)
    copies = {
        m.name: remote(m.ref, m.ref, gsend.at[n], grecv.at[n], target(me, m)) for n, m in enumerate(plan)
    }

    def prepare(part):
        if part == 0:
            loads[4].wait()
            loads[5].wait()
            swap.wait()

        @pl.loop(part * 4, part * 4 + 4)
        def _(k):
            cols = pl.ds(pl.multiple_of(k * 512, 512), 512)
            high, low = split(raw[:, cols] * inv[:, cols])
            st_hi[:, cols] = high
            st_lo[:, cols] = low

    def outer(r, part):
        by = (y + r) % NY
        high_at = NEAR.index(r) * 64 if r != FAR else 384
        low_at = high_at + (192 if r != FAR else 64)

        @pl.loop(part * 2, part * 2 + 2)
        def _(bz):
            g = split(grads[by, bz].reshape(512, 256))
            mine = ins[by, bz]
            rows = jnp.concatenate([mine[32 * k:32 * k + 32] for k in range(4)], axis=1)
            slot = jnp.concatenate([mine[128 + k:129 + k] for k in range(4)], axis=1)
            member = (slot == lax.broadcasted_iota(jnp.int32, (QB, 512), 0).astype(F32)).astype(F32)
            high = rows.astype(BF16).astype(F32)
            masked = [
                (v[:, None, :] * member[None]).reshape(512, 512).astype(BF16) for v in (high, rows - high)
            ]
            high, low = split(dot3(masked, g, (((1,), (0,)), ((), ()))))
            for i in range(32):
                cols = slice(i * 256, (i + 1) * 256)
                q[pl.ds(pl.multiple_of(high_at + bz * QB, QB), QB), cols] = high[i * QB:(i + 1) * QB]
                q[pl.ds(pl.multiple_of(low_at + bz * QB, QB), QB), cols] = low[i * QB:(i + 1) * QB]

    last = (((1,), (1,)), ((), ()))

    def near_scores(part):
        if part == 0:
            sc[...] = jnp.zeros_like(sc)

        @pl.loop(part * 2, part * 2 + 2)
        def _(k):
            cols = pl.ds(pl.multiple_of(k * 1024, 1024), 1024)
            both = lax.dot_general(q[0:384, cols], st_hi[:, cols], last, preferred_element_type=F32)
            high = lax.dot_general(q[0:192, cols], st_lo[:, cols], last, preferred_element_type=F32)
            total = both[0:192] + both[192:384] + high
            for n, r in enumerate(NEAR):
                to = (y + r) % NX
                sc[to] = sc[to] + total[n * 64:(n + 1) * 64].reshape(2, 32, 384)

    def far_scores():
        def step(k, total):
            cols = pl.ds(pl.multiple_of(k * 1024, 1024), 1024)
            both = lax.dot_general(st_hi[:, cols], q[384:512, cols], last, preferred_element_type=F32)
            high = lax.dot_general(st_lo[:, cols], q[384:448, cols], last, preferred_element_type=F32)
            return total[0] + both, total[1] + high

        both, high = lax.fori_loop(0, 8, step, (jnp.zeros((384, 128), F32), jnp.zeros((384, 64), F32)))
        rows = (both[:, 0:64] + both[:, 64:128] + high).T
        sc[(y + FAR) % NX] = rows.reshape(2, 32, 384)

    def pass_on(r):
        to = (y + r) % NX
        slot = (x - to + NX - 1) % NX

        @pl.when(to != x)
        def _():
            remote(sc.at[to], rsc.at[slot], ssend.at[slot], srecv.at[slot], device(to, y, z, c)).start()

    tasks = [(f"prepare{n}", ("A0z1",), 0.6) for n in range(4)]
    run = {f"prepare{n}": (prepare, (n,)) for n in range(4)}
    done = [f"prepare{n}" for n in range(4)]
    for r in NEAR:
        for n in range(2):
            tasks.append((f"outer{r},{n}", tuple(needs[r]), 1.3))
            run[f"outer{r},{n}"] = (outer, (r, n))
            done.append(f"outer{r},{n}")
    for n in range(4):
        tasks.append((f"near{n}", tuple(done), 1.5))
        run[f"near{n}"] = (near_scores, (n,))
        done.append(f"near{n}")
    for r in NEAR:
        tasks.append((f"pass{r}", tuple(done) + tuple(needs[FAR]), 0.1))
        run[f"pass{r}"] = (pass_on, (r,))
    for n in range(2):
        tasks.append((f"outer{FAR},{n}", tuple(done) + tuple(needs[FAR]), 1.3))
        run[f"outer{FAR},{n}"] = (outer, (FAR, n))

    for verb, name in order_of(plan, tasks)[0]:
        if name == "gc":
            first["Zc"].wait_recv()
            grads[y, zlo, x, zhi, early] = pg[x, zhi, early] + rg[6, early]
        elif name == "g":
            first["Z"].wait_recv()
            grads[y, zlo, x, zhi, later] = pg[x, zhi, later] + rg[6, later]
        elif name == "i":
            second["Z"].wait_recv()
            whole = pin[x, zhi] + rin[6]
            for k in range(4):
                ins[y, zlo, 32 * k:32 * k + 32, :] = whole[:, 128 * k:128 * k + 128]
        elif verb == "send":
            copies[name].start()
        elif verb == "wait":
            copies[name].wait_recv()
        else:
            work, given = run[name]
            work(*given)
    far_scores()
    pass_on(FAR)
    for copy in (*first.values(), *second.values(), *copies.values()):
        copy.wait_send()

    sends = [
        remote(sc.at[x], rsc.at[n], ssend.at[n], srecv.at[n], right) for n in range(3)
    ]
    for copy in sends:
        copy.wait_recv()
    sc[x] = sc[x] + (rsc[0] + rsc[1]) + rsc[2]
    ours, others = (pl.ds(pl.multiple_of(k * 128, 128), 256) for k in (c, 1 - c))
    ends = [
        remote(sc.at[x, 1 - zhi, :, ours], fin.at[0], fsend.at[0], frecv.at[0], device(x, y, z + 4, c)),
        remote(sc.at[x, 1 - zhi, :, others], fin.at[1], fsend.at[1], frecv.at[1], device(x, y, z + 4, c + 1)),
        remote(sc.at[x, zhi, :, others], fin.at[2], fsend.at[2], frecv.at[2], core),
    ]
    for copy in ends:
        copy.start()
    for copy in ends:
        copy.wait_recv()
    mine, theirs = (
        jnp.where(c == 0, v[:, 0:192], v[:, 64:256])
        for v in (sc[x, zhi, :, ours] + fin[0], fin[1] + fin[2])
    )
    for half in range(2):
        part = slice(half * QB, (half + 1) * QB)
        out_ref[pl.ds(pl.multiple_of(half * 32 + c * QB, QB), QB), :] = mine[part]
        out_ref[pl.ds(pl.multiple_of(half * 32 + (1 - c) * QB, QB), QB), :] = theirs[part]

    for copy in (*sends, *ends):
        copy.wait_send()


def body(layer_input, out_grad, proj_in, proj_out, inv_diag, stored, seq_lengths, query_order):
    hbm, smem = pl.BlockSpec(memory_space=pl.ANY), pl.BlockSpec(memory_space=pltpu.SMEM)
    dma = pltpu.SemaphoreType.DMA
    return pl.pallas_call(
        kernel,
        out_shape=jax.ShapeDtypeStruct((64, 192), F32),
        in_specs=[hbm] * 6 + [smem] * 2,
        out_specs=pl.BlockSpec(memory_space=pltpu.VMEM),
        scratch_shapes=[
            pltpu.VMEM((512, 1024), BF16),
            pltpu.VMEM((512, 1024), BF16),
            pltpu.VMEM((1024, 256), BF16),
            pltpu.VMEM((1024, 256), BF16),
            pltpu.VMEM((1, 8192), F32),
            pltpu.VMEM((384, 8192), F32),
            pltpu.VMEM((384, 8192), BF16),
            pltpu.VMEM((384, 8192), BF16),
            pltpu.VMEM((4, 2, 64, 256), F32),
            pltpu.VMEM((4, 2, 32, 512), F32),
            pltpu.VMEM((7, 64, 256), F32),
            pltpu.VMEM((7, 32, 512), F32),
            pltpu.VMEM((4, 4, 4, 2, TOK, 256), F32),
            pltpu.VMEM((4, 4, INROWS, 128), F32),
            pltpu.VMEM((512, 8192), BF16),
            pltpu.VMEM((4, 2, 32, 384), F32),
            pltpu.VMEM((3, 2, 32, 384), F32),
            pltpu.VMEM((3, 32, 256), F32),
            dma((6,)),
            dma((176,)), dma((176,)),
            dma((2, 8)), dma((2, 8)),
            dma((3,)), dma((3,)),
            dma((4,)), dma((4,)),
        ],
        compiler_params=pltpu.CompilerParams(
            collective_id=0, has_side_effects=True, vmem_limit_bytes=60 * 2**20
        ),
    )(layer_input, out_grad, proj_in, proj_out, inv_diag.reshape(1, -1), stored, seq_lengths, query_order)


def solution(mesh):
    return jax.shard_map(
        body,
        mesh=mesh,
        in_specs=(
            P("store", "feat"),
            P("store", "feat"),
            P("feat", None),
            P("feat", None),
            P("feat"),
            P("store", "feat"),
            P("store", None),
            P("store", None),
        ),
        out_specs=P("feat", "store"),
        check_vma=False,
    )
```
